128 devices in a mesh: gx: 32 (over z, x, core), yz: 4 (over y).
Axes of the slice: x: 4, y: 4, z: 4, core: 2. Of those that a mesh axis runs over, the one named last changes fastest.
Arguments:
- residuals: float32 [32, 3, 256, 32, 128], P(None, None, 'gx', 'yz'), may hold values from -6 to 6
- vectors: float32 [8, 3, 256, 32, 128], P(None, None, 'gx', 'yz'), may hold values from -0.05 to 1.6
- phases: int32 [256, 32, 128], P('gx', 'yz'), may hold values from 0 to 7
- stiffness: float32 [8], replicated, may hold values from 0.5 to 4
Outputs:
- coarse_coeffs: float32 [1024, 32], P(('gx', 'yz'))
- preconditioned: float32 [32, 3, 256, 32, 128], P(None, None, 'gx', 'yz')
The draws below stay inside these ranges and needn't reach their ends.
All inputs are finite; a program needn't handle non-finite values.
Results may differ from the reference program's by a relative error of at most 0.0003.
Values sent between devices are 32-bit elements; how exact they have to be, the bound alone decides.
No kernel may reach another device: no remote copies, remote signals or barrier semaphores. Data moves between devices by JAX's collectives and lax.ppermute only.
A program may use at most 192 MiB of HBM per device.

```python
import math
import jax
import jax.numpy as jnp
from jax import lax

K = 8
PHASES = 8
CX = 8
CY = 8
CZ = 128
RHS = 32
SWEEPS = 4
NX = 256
NY = 32
N_GX = 32
N_YZ = 4


def draw_vectors(key, part):
    first_key, second_key = jax.random.split(jax.random.fold_in(key, 17))
    means = jax.random.uniform(first_key, (K, 3, 1, 1, 1), jnp.float32, 0.2, 1.0)
    rough = jnp.clip(0.05 * jax.random.normal(second_key, (K, 3, NX, NY, CZ), jnp.float32), -0.25, 0.25)
    return means + rough


def set_ends(result, rng, smallest, top_value):
    spot = [jax.random.randint(jax.random.fold_in(rng, axis), (), 0, length) for axis, length in enumerate(result.shape)]
    main_axis = result.shape.index(max(result.shape))
    next_to = spot[:main_axis] + [(spot[main_axis] + 1) % result.shape[main_axis]] + spot[main_axis + 1:]
    return result.at[tuple(spot)].set(smallest).at[tuple(next_to)].set(top_value)


def level_of(own_key, shape, cuts, smallest, top_value):
    factor_of, own = 1.0, jax.random.fold_in(own_key, 6)
    for dim, blocks in cuts:
        steps = jnp.exp(jax.random.uniform(jax.random.fold_in(own, dim), (blocks,), jnp.float32, smallest / len(cuts), top_value / len(cuts)))
        factor_of = factor_of * jnp.repeat(steps, shape[dim] // blocks).reshape([-1 if axis == dim else 1 for axis in range(len(shape))])
    return factor_of


def scatter_about(rng, dims, deviation, limit, shards=(), held_as=jnp.bfloat16):
    drawn = jax.random.normal(rng, dims, jnp.float32) * deviation
    if len(shards) > 0:
        drawn = level_of(rng, dims, shards, -0.22, 0.18) * drawn
    return jnp.clip(drawn, min=-limit, max=limit).astype(held_as)


def setup_inputs(seed: int = 0) -> dict:
    arg_keys = jax.random.split(jax.random.key(seed), 5)
    return {
        "residuals": scatter_about(arg_keys[0], (RHS, 3, NX, NY, CZ), 1.0, 6.0, ((2, 32), (3, 4)), jnp.float32),
        "vectors": draw_vectors(jax.random.fold_in(arg_keys[4], 71), 0),
        "phases": set_ends(jax.random.randint(arg_keys[2], (NX, NY, CZ), 0, PHASES), jax.random.fold_in(arg_keys[2], 1), 0, PHASES - 1).astype(jnp.int32),
        "stiffness": jnp.clip(jnp.exp(jax.random.uniform(arg_keys[3], (PHASES,), jnp.float32, math.log(0.5), math.log(4.0))), 0.5, 4.0),
    }


HIGH = lax.Precision.HIGHEST

def face_weights(modulus_ext):
    centre = modulus_ext[1:-1, 1:-1, :]
    zpadded = jnp.pad(centre, ((0, 0), (0, 0), (1, 1)))
    west_side = 0.5 * (centre + modulus_ext[:-2, 1:-1, :])
    east_side = 0.5 * (centre + modulus_ext[2:, 1:-1, :])
    south_side = 0.5 * (centre + modulus_ext[1:-1, :-2, :])
    north_side = 0.5 * (centre + modulus_ext[1:-1, 2:, :])
    lower_side = 0.5 * (centre + zpadded[:, :, :-2])
    upper_side = 0.5 * (centre + zpadded[:, :, 2:])
    diagonal_sum = 0.002 + west_side + east_side + south_side + north_side + lower_side + upper_side
    return (diagonal_sum, west_side, east_side, south_side, north_side, lower_side, upper_side)

def operate(values, weights):
    diagonal_sum, west_side, east_side, south_side, north_side, lower_side, upper_side = weights
    centre = values[..., 1:-1, 1:-1, :]
    spacing = [(0, 0)] * (values.ndim - 1) + [(1, 1)]
    zpadded = jnp.pad(centre, spacing)
    beside = west_side * values[..., :-2, 1:-1, :] + east_side * values[..., 2:, 1:-1, :]
    beside = beside + south_side * values[..., 1:-1, :-2, :] + north_side * values[..., 1:-1, 2:, :]
    beside = beside + lower_side * zpadded[..., :-2] + upper_side * zpadded[..., 2:]
    return diagonal_sum * centre - beside

def coarse_blocks(vectors_ext, modulus_ext):
    weights = face_weights(modulus_ext[1:-1, 1:-1, :])
    own_cells = vectors_ext[:, :, 2:-2, 2:-2, :]
    isolated = jnp.pad(own_cells, ((0, 0), (0, 0), (1, 1), (1, 1), (0, 0)))
    applied = operate(isolated, weights)
    self_block = jnp.einsum('kcxyz,lcxyz->kl', own_cells, applied, precision=HIGH)
    west_block = -jnp.einsum('kcyz,lcyz->kl', weights[1][0] * own_cells[:, :, 0], vectors_ext[:, :, 1, 2:-2, :], precision=HIGH)
    east_block = -jnp.einsum('kcyz,lcyz->kl', weights[2][-1] * own_cells[:, :, -1], vectors_ext[:, :, -2, 2:-2, :], precision=HIGH)
    south_block = -jnp.einsum('kcxz,lcxz->kl', weights[3][:, 0] * own_cells[:, :, :, 0], vectors_ext[:, :, 2:-2, 1, :], precision=HIGH)
    north_block = -jnp.einsum('kcxz,lcxz->kl', weights[4][:, -1] * own_cells[:, :, :, -1], vectors_ext[:, :, 2:-2, -2, :], precision=HIGH)
    return jnp.stack([self_block, west_block, east_block, south_block, north_block])

def assemble(blocks, stride):
    count = blocks.shape[0]
    width = blocks.shape[2]
    rows_index = jnp.arange(count, dtype=jnp.int32)
    assembled = jnp.zeros((count, width, count, width), jnp.float32)
    for slot_index, offset in enumerate((0, -stride, stride, -1, 1)):
        select = (rows_index[None, :] == rows_index[:, None] + offset).astype(jnp.float32)
        assembled = assembled + blocks[:, slot_index][:, :, None, :] * select[:, None, :, None]
    return assembled.reshape(count * width, count * width)

def local_solve(deflated_ext, modulus_ext):
    weights = face_weights(modulus_ext)
    inner_mod = modulus_ext[1:-1, 1:-1, :]
    width_x = inner_mod.shape[0]
    width_y = inner_mod.shape[1]
    x_index = jnp.arange(width_x)[:, None]
    y_index = jnp.arange(width_y)[None, :]
    x_edge = (x_index == 0) | (x_index == width_x - 1)
    y_edge = (y_index == 0) | (y_index == width_y - 1)
    corner = x_edge & y_edge
    active = ((inner_mod > 0) & jnp.logical_not(corner[:, :, None])).astype(jnp.float32)
    approx = jnp.zeros_like(deflated_ext)
    for repeat in range(SWEEPS):
        padded = jnp.pad(approx, ((0, 0), (0, 0), (1, 1), (1, 1), (0, 0)))
        approx = active * (approx + 0.8 * (deflated_ext - operate(padded, weights)) / weights[0])
    return approx[:, :, 1:-1, 1:-1, :]

def reference(residuals, vectors, phases, stiffness):
    count = N_GX * N_YZ
    modulus = jnp.take(stiffness, phases, axis=0)
    modulus_pad = jnp.pad(modulus, ((2, 2), (2, 2), (0, 0)))
    vectors_pad = jnp.pad(vectors, ((0, 0), (0, 0), (2, 2), (2, 2), (0, 0)))
    zero_index = jnp.zeros((), jnp.int32)
    block_ids = jnp.arange(count, dtype=jnp.int32)

    def starts(block_index):
        x_start = (block_index // N_YZ * CX).astype(jnp.int32)
        y_start = (block_index % N_YZ * CY).astype(jnp.int32)
        return (x_start, y_start)

    def coarse_part(block_index):
        x_start, y_start = starts(block_index)
        modulus_ext = lax.dynamic_slice(modulus_pad, (x_start, y_start, zero_index), (CX + 4, CY + 4, CZ))
        vectors_ext = lax.dynamic_slice(vectors_pad, (zero_index, zero_index, x_start, y_start, zero_index), (K, 3, CX + 4, CY + 4, CZ))
        own_res = lax.dynamic_slice(residuals, (zero_index, zero_index, x_start, y_start, zero_index), (RHS, 3, CX, CY, CZ))
        own_vec = vectors_ext[:, :, 2:-2, 2:-2, :]
        rhs_part = jnp.einsum('kcxyz,rcxyz->kr', own_vec, own_res, precision=HIGH)
        return (coarse_blocks(vectors_ext, modulus_ext), rhs_part)
    blocks, rhs_parts = lax.map(coarse_part, block_ids)
    matrix = assemble(blocks, N_YZ)
    coarse_rhs = rhs_parts.reshape(count * K, RHS)
    factor = jnp.linalg.cholesky(matrix)
    coarse_coeffs = jax.scipy.linalg.cho_solve((factor, True), coarse_rhs)
    coeff_grid = coarse_coeffs.reshape(N_GX, N_YZ, K, RHS)
    vector_grid = vectors.reshape(K, 3, N_GX, CX, N_YZ, CY, CZ)
    correction = jnp.einsum('gqkr,kcgaqbz->rcgaqbz', coeff_grid, vector_grid, precision=HIGH).reshape(RHS, 3, NX, NY, CZ)
    corr_pad = jnp.pad(correction, ((0, 0), (0, 0), (2, 2), (2, 2), (0, 0)))
    res_pad = jnp.pad(residuals, ((0, 0), (0, 0), (1, 1), (1, 1), (0, 0)))

    def local_block(block_index):
        x_start, y_start = starts(block_index)
        modulus_ext = lax.dynamic_slice(modulus_pad, (x_start, y_start, zero_index), (CX + 4, CY + 4, CZ))
        corr_ext = lax.dynamic_slice(corr_pad, (zero_index, zero_index, x_start, y_start, zero_index), (RHS, 3, CX + 4, CY + 4, CZ))
        res_ext = lax.dynamic_slice(res_pad, (zero_index, zero_index, x_start, y_start, zero_index), (RHS, 3, CX + 2, CY + 2, CZ))
        deflated_ext = res_ext - operate(corr_ext, face_weights(modulus_ext))
        local_part = local_solve(deflated_ext, modulus_ext)
        return corr_ext[:, :, 2:-2, 2:-2, :] + local_part
    pieces = lax.map(local_block, block_ids)
    preconditioned = pieces.reshape(N_GX, N_YZ, RHS, 3, CX, CY, CZ).transpose(2, 3, 0, 4, 1, 5, 6).reshape(RHS, 3, NX, NY, CZ)
    return (coarse_coeffs, preconditioned)
```

```python
import functools
import jax
import jax.numpy as jnp
from jax import lax
from jax.experimental import pallas as pl
from jax.experimental.pallas import tpu as pltpu
from jax.sharding import PartitionSpec as P

SWEEPS = 4


HIGH = lax.Precision.HIGHEST


def extended(cells, sides, width):
    for axis, dim in sides:
        count = lax.axis_size(axis)
        ends = count - 1
        head = lax.slice_in_dim(cells, 0, width, axis=dim)
        tail = lax.slice_in_dim(cells, cells.shape[dim] - width, cells.shape[dim], axis=dim)
        cells = jnp.concatenate(
            [
                lax.ppermute(tail, axis, [(i, (i + 1) % count) for i in range(ends)]),
                cells,
                lax.ppermute(head, axis, [((i + 1) % count, i) for i in range(ends)]),
            ],
            axis=dim,
        )
    return cells


def face_weights(modulus_ext):
    centre = modulus_ext[1:-1, 1:-1, :]
    zpadded = jnp.pad(centre, ((0, 0), (0, 0), (1, 1)))
    west_side = 0.5 * (centre + modulus_ext[:-2, 1:-1, :])
    east_side = 0.5 * (centre + modulus_ext[2:, 1:-1, :])
    south_side = 0.5 * (centre + modulus_ext[1:-1, :-2, :])
    north_side = 0.5 * (centre + modulus_ext[1:-1, 2:, :])
    lower_side = 0.5 * (centre + zpadded[:, :, :-2])
    upper_side = 0.5 * (centre + zpadded[:, :, 2:])
    diagonal_sum = 0.002 + west_side + east_side + south_side + north_side + lower_side + upper_side
    return (diagonal_sum, west_side, east_side, south_side, north_side, lower_side, upper_side)


def operate(values, weights):
    diagonal_sum, west_side, east_side, south_side, north_side, lower_side, upper_side = weights
    centre = values[..., 1:-1, 1:-1, :]
    spacing = [(0, 0)] * (values.ndim - 1) + [(1, 1)]
    zpadded = jnp.pad(centre, spacing)
    beside = west_side * values[..., :-2, 1:-1, :] + east_side * values[..., 2:, 1:-1, :]
    beside = beside + south_side * values[..., 1:-1, :-2, :] + north_side * values[..., 1:-1, 2:, :]
    beside = beside + lower_side * zpadded[..., :-2] + upper_side * zpadded[..., 2:]
    return diagonal_sum * centre - beside


def coarse_blocks(vectors_ext, modulus_ext):
    weights = face_weights(modulus_ext[1:-1, 1:-1, :])
    own_cells = vectors_ext[:, :, 2:-2, 2:-2, :]
    isolated = jnp.pad(own_cells, ((0, 0), (0, 0), (1, 1), (1, 1), (0, 0)))
    applied = operate(isolated, weights)
    self_block = jnp.einsum("kcxyz,lcxyz->kl", own_cells, applied, precision=HIGH)
    west_block = -jnp.einsum(
        "kcyz,lcyz->kl",
        weights[1][0] * own_cells[:, :, 0],
        vectors_ext[:, :, 1, 2:-2, :],
        precision=HIGH,
    )
    east_block = -jnp.einsum(
        "kcyz,lcyz->kl",
        weights[2][-1] * own_cells[:, :, -1],
        vectors_ext[:, :, -2, 2:-2, :],
        precision=HIGH,
    )
    south_block = -jnp.einsum(
        "kcxz,lcxz->kl",
        weights[3][:, 0] * own_cells[:, :, :, 0],
        vectors_ext[:, :, 2:-2, 1, :],
        precision=HIGH,
    )
    north_block = -jnp.einsum(
        "kcxz,lcxz->kl",
        weights[4][:, -1] * own_cells[:, :, :, -1],
        vectors_ext[:, :, 2:-2, -2, :],
        precision=HIGH,
    )
    return jnp.stack([self_block, west_block, east_block, south_block, north_block])


def eliminate(work, picks, size):
    lanes = lax.broadcasted_iota(jnp.int32, (size, 128), 0)

    def pivot(j, carry):
        index = jnp.full((size, 128), j, jnp.int32)
        for pick in picks:
            block = work[pick]
            row = jnp.broadcast_to(work[pick, pl.ds(j, 1), :], (size, 128))
            scaled = row / jnp.take_along_axis(row, index, axis=1)
            column = jnp.take_along_axis(block, index, axis=1)
            work[pick] = jnp.where(lanes == j, scaled, block - column * scaled)
        return carry

    lax.fori_loop(0, size, pivot, 0)


def coarse_solve(slabs, size, rows_ref, out_ref, work, found):
    work[...] = rows_ref[...]
    lane = lax.broadcasted_iota(jnp.int32, (size, 128), 1)
    level = 1
    steps = []
    while level < slabs:
        picks = list(range(level, slabs, 2 * level))
        steps.append((level, picks))
        eliminate(work, picks, size)
        for keep in range(0, slabs, 2 * level):
            own = work[keep]
            left, right = keep - level, keep + level
            parts = [jnp.zeros((size, 128), jnp.float32)]
            if left >= 0:
                block = work[left]
                moved = pltpu.roll(block, 128 - 2 * size, 1)
                taken = jnp.where(lane < size, moved, jnp.where((lane >= 2 * size) & (lane < 3 * size), 0.0, block))
                parts.append(taken)
            else:
                parts.append(jnp.zeros((size, 128), jnp.float32))
            if right < slabs:
                block = work[right]
                moved = pltpu.roll(block, 128 - size, 1)
                taken = jnp.where(lane < size, moved, jnp.where((lane >= size) & (lane < 2 * size), 0.0, block))
                parts.append(taken)
            else:
                parts.append(jnp.zeros((size, 128), jnp.float32))
            parts.append(jnp.zeros((size, 128), jnp.float32))
            change = jnp.dot(own, jnp.concatenate(parts, axis=0), precision=HIGH, preferred_element_type=jnp.float32)
            kept = jnp.where((lane >= size) & (lane < 3 * size), 0.0, own)
            work[keep] = kept - change
        level *= 2
    eliminate(work, [0], size)
    zeros = jnp.zeros((size, 128), jnp.float32)
    found[0] = jnp.where(lane >= 3 * size, work[0], 0.0)
    unit = jnp.where(lane - 3 * size == lax.broadcasted_iota(jnp.int32, (size, 128), 0), 1.0, 0.0)
    for level, picks in reversed(steps):
        for pick in picks:
            left = -found[pick - level]
            right = -found[pick + level] if pick + level < slabs else zeros
            stack = jnp.concatenate([zeros, left, right, unit], axis=0)
            found[pick] = jnp.dot(work[pick], stack, precision=HIGH, preferred_element_type=jnp.float32)
    out_ref[...] = found[:, :, 3 * size :].reshape(slabs * size, 128 - 3 * size)


def solve_rows(rows, slabs, size):
    shape = (slabs, size, 128)
    return pl.pallas_call(
        functools.partial(coarse_solve, slabs, size),
        out_shape=jax.ShapeDtypeStruct((slabs * size, 128 - 3 * size), jnp.float32),
        scratch_shapes=[pltpu.VMEM(shape, jnp.float32), pltpu.VMEM(shape, jnp.float32)],
        compiler_params=pltpu.CompilerParams(vmem_limit_bytes=16 * 1024 * 1024),
    )(rows.reshape(shape))


def coarse_rows(blocks, coarse_rhs, spot, count):
    width = blocks.shape[1]
    columns = jnp.arange(count, dtype=jnp.int32)

    def placed(*parts):
        panel = jnp.zeros((width, count, width), jnp.float32)
        for block, offset in parts:
            select = (columns == spot + offset).astype(jnp.float32)
            panel = panel + block[:, None, :] * select[None, :, None]
        return panel.reshape(width, count * width)

    return jnp.concatenate(
        [
            placed((blocks[0], 0), (blocks[3], -1), (blocks[4], 1)),
            placed((blocks[1], 0)),
            placed((blocks[2], 0)),
            coarse_rhs,
        ],
        axis=1,
    )


def neighbour_field(coeffs_all, width, count_x, count_y, size_x, size_y):
    index_x = lax.axis_index("gx")
    index_y = lax.axis_index("yz")
    rows_list = []
    for step_x in (-1, 0, 1):
        cols_list = []
        for step_y in (-1, 0, 1):
            near_x = jnp.clip(index_x + step_x, 0, count_x - 1)
            near_y = jnp.clip(index_y + step_y, 0, count_y - 1)
            start = (near_x * count_y + near_y) * width
            cols_list.append(lax.dynamic_slice_in_dim(coeffs_all, start, width, 0))
        rows_list.append(jnp.stack(cols_list))
    coeff_grid = jnp.stack(rows_list)
    cells_x = jnp.arange(size_x + 4, dtype=jnp.int32)
    cells_y = jnp.arange(size_y + 4, dtype=jnp.int32)
    class_x = (cells_x >= 2).astype(jnp.int32) + (cells_x >= size_x + 2).astype(jnp.int32)
    class_y = (cells_y >= 2).astype(jnp.int32) + (cells_y >= size_y + 2).astype(jnp.int32)
    three = jnp.arange(3, dtype=jnp.int32)
    onehot_x = (class_x[:, None] == three[None, :]).astype(jnp.float32)
    onehot_y = (class_y[:, None] == three[None, :]).astype(jnp.float32)
    return jnp.einsum("xa,yb,abkr->krxy", onehot_x, onehot_y, coeff_grid, precision=HIGH)


def local_solve(deflated_ext, modulus_ext):
    weights = face_weights(modulus_ext)
    inner_mod = modulus_ext[1:-1, 1:-1, :]
    width_x = inner_mod.shape[0]
    width_y = inner_mod.shape[1]
    x_index = jnp.arange(width_x)[:, None]
    y_index = jnp.arange(width_y)[None, :]
    x_edge = (x_index == 0) | (x_index == width_x - 1)
    y_edge = (y_index == 0) | (y_index == width_y - 1)
    corner = x_edge & y_edge
    active = ((inner_mod > 0) & jnp.logical_not(corner[:, :, None])).astype(jnp.float32)
    approx = jnp.zeros_like(deflated_ext)
    for repeat in range(SWEEPS):
        padded = jnp.pad(approx, ((0, 0), (0, 0), (1, 1), (1, 1), (0, 0)))
        approx = active * (approx + 0.8 * (deflated_ext - operate(padded, weights)) / weights[0])
    return approx[:, :, 1:-1, 1:-1, :]


def on_device(residuals, vectors, phases, stiffness):
    count_x = lax.axis_size("gx")
    count_y = lax.axis_size("yz")
    count = count_x * count_y
    position = lax.axis_index("gx") * count_y + lax.axis_index("yz")
    width = vectors.shape[0]
    levels = stiffness.shape[0]
    choose = (phases[None] == jnp.arange(levels, dtype=jnp.int32)[:, None, None, None]).astype(
        jnp.float32
    )
    modulus = jnp.sum(stiffness[:, None, None, None] * choose, axis=0)
    vectors_ext, modulus_wide = (
        extended(vectors, (("gx", 2), ("yz", 3)), 2),
        extended(modulus[None, None], (("gx", 2), ("yz", 3)), 2),
    )
    modulus_ext = modulus_wide[0, 0]
    residual_near = extended(residuals, (("gx", 2), ("yz", 3)), 1)
    blocks = coarse_blocks(vectors_ext, modulus_ext)
    coarse_rhs = jnp.einsum("kcxyz,rcxyz->kr", vectors, residuals, precision=HIGH)
    own_rows = coarse_rows(blocks, coarse_rhs, lax.axis_index("yz"), count_y)
    every = jnp.broadcast_to(own_rows[None], (count,) + own_rows.shape)
    rows = lax.all_to_all(every, ("gx", "yz"), 0, 0)
    coeffs_all = solve_rows(rows, count_x, count_y * width)
    coeffs = lax.dynamic_slice_in_dim(coeffs_all, position * width, width, 0)
    correction = jnp.einsum("kr,kcxyz->rcxyz", coeffs, vectors, precision=HIGH)
    coeff_field = neighbour_field(
        coeffs_all, width, count_x, count_y, vectors.shape[2], vectors.shape[3]
    )
    corr_ext = jnp.einsum("krxy,kcxyz->rcxyz", coeff_field, vectors_ext, precision=HIGH)
    deflated_ext = residual_near - operate(corr_ext, face_weights(modulus_ext))
    local_part = local_solve(deflated_ext, modulus_ext)
    return (coeffs, correction + local_part)


def solution(mesh):
    return jax.shard_map(
        on_device,
        mesh=mesh,
        in_specs=(
            P(None, None, "gx", "yz", None),
            P(None, None, "gx", "yz", None),
            P("gx", "yz", None),
            P(),
        ),
        out_specs=(P(("gx", "yz"), None), P(None, None, "gx", "yz", None)),
        check_vma=False,
    )
```

```python
import functools
import jax
import jax.numpy as jnp
from jax import lax
from jax.experimental import pallas as pl
from jax.experimental.pallas import tpu as pltpu
from jax.sharding import PartitionSpec as P

HIGH = lax.Precision.HIGHEST


def face_weights(modulus_ext):
    centre = modulus_ext[1:-1, 1:-1, :]
    zpadded = jnp.pad(centre, ((0, 0), (0, 0), (1, 1)))
    west_side = 0.5 * (centre + modulus_ext[:-2, 1:-1, :])
    east_side = 0.5 * (centre + modulus_ext[2:, 1:-1, :])
    south_side = 0.5 * (centre + modulus_ext[1:-1, :-2, :])
    north_side = 0.5 * (centre + modulus_ext[1:-1, 2:, :])
    lower_side = 0.5 * (centre + zpadded[:, :, :-2])
    upper_side = 0.5 * (centre + zpadded[:, :, 2:])
    diagonal_sum = 0.002 + west_side + east_side + south_side + north_side + lower_side + upper_side
    return (diagonal_sum, west_side, east_side, south_side, north_side, lower_side, upper_side)


def operate(values, weights):
    diagonal_sum, west_side, east_side, south_side, north_side, lower_side, upper_side = weights
    centre = values[..., 1:-1, 1:-1, :]
    spacing = [(0, 0)] * (values.ndim - 1) + [(1, 1)]
    zpadded = jnp.pad(centre, spacing)
    beside = west_side * values[..., :-2, 1:-1, :] + east_side * values[..., 2:, 1:-1, :]
    beside = beside + south_side * values[..., 1:-1, :-2, :] + north_side * values[..., 1:-1, 2:, :]
    beside = beside + lower_side * zpadded[..., :-2] + upper_side * zpadded[..., 2:]
    return diagonal_sum * centre - beside


def coarse_blocks(vectors_ext, modulus_ext):
    weights = face_weights(modulus_ext[1:-1, 1:-1, :])
    own_cells = vectors_ext[:, :, 2:-2, 2:-2, :]
    isolated = jnp.pad(own_cells, ((0, 0), (0, 0), (1, 1), (1, 1), (0, 0)))
    applied = operate(isolated, weights)
    self_block = jnp.einsum("kcxyz,lcxyz->kl", own_cells, applied, precision=HIGH)
    west_block = -jnp.einsum(
        "kcyz,lcyz->kl",
        weights[1][0] * own_cells[:, :, 0],
        vectors_ext[:, :, 1, 2:-2, :],
        precision=HIGH,
    )
    east_block = -jnp.einsum(
        "kcyz,lcyz->kl",
        weights[2][-1] * own_cells[:, :, -1],
        vectors_ext[:, :, -2, 2:-2, :],
        precision=HIGH,
    )
    south_block = -jnp.einsum(
        "kcxz,lcxz->kl",
        weights[3][:, 0] * own_cells[:, :, :, 0],
        vectors_ext[:, :, 2:-2, 1, :],
        precision=HIGH,
    )
    north_block = -jnp.einsum(
        "kcxz,lcxz->kl",
        weights[4][:, -1] * own_cells[:, :, :, -1],
        vectors_ext[:, :, 2:-2, -2, :],
        precision=HIGH,
    )
    return jnp.stack([self_block, west_block, east_block, south_block, north_block])


def spread(values, column):
    return jnp.broadcast_to(values[:, column : column + 1], values.shape)


def eliminate(work, picks, groups):
    row_index = lax.broadcasted_iota(jnp.int32, (8, 128), 0)

    def turn(step, carry):
        mats = [[work[pick, 8 * i : 8 * i + 8, :] for i in range(groups)] for pick in picks]
        for j in range(0, 8, 2):
            for mat in mats:
                top = mat[0]
                row0 = jnp.broadcast_to(top[j : j + 1, :], (8, 128))
                row1 = jnp.broadcast_to(top[j + 1 : j + 2, :], (8, 128))
                a, b = spread(row0, j), spread(row0, j + 1)
                c, d = spread(row1, j), spread(row1, j + 1)
                inverse = 1.0 / (a * d - b * c)
                new0 = (d * row0 - b * row1) * inverse
                new1 = (a * row1 - c * row0) * inverse
                for i in range(groups):
                    changed = mat[i] - spread(mat[i], j) * new0 - spread(mat[i], j + 1) * new1
                    if i == 0:
                        changed = jnp.where(row_index == j, new0, jnp.where(row_index == j + 1, new1, changed))
                    mat[i] = changed
        for pick, mat in zip(picks, mats):
            for i in range(groups):
                to = (i + groups - 1) % groups
                work[pick, 8 * to : 8 * to + 8, :] = pltpu.roll(mat[i], 120, 1)
        return carry

    lax.fori_loop(0, groups, turn, 0)


def coarse_solve(slabs, size, chunk, rows_ref, out_ref, work, found):
    work[...] = rows_ref[...]
    lane = lax.broadcasted_iota(jnp.int32, (size, 128), 1)
    zeros = jnp.zeros((size, 128), jnp.float32)
    level = 1
    steps = []
    while level < slabs:
        picks = list(range(level, slabs, 2 * level))
        steps.append((level, picks))
        for at in range(0, len(picks), chunk):
            eliminate(work, picks[at : at + chunk], size // 8)
        for keep in range(0, slabs, 2 * level):
            own = work[keep]
            left, right = keep - level, keep + level
            before, after = zeros, zeros
            if left >= 0:
                block = work[left]
                before = jnp.where(
                    lane < size,
                    pltpu.roll(block, 128 - size, 1),
                    jnp.where((lane >= 2 * size) & (lane < 3 * size), 0.0, pltpu.roll(block, size, 1)),
                )
            if right < slabs:
                block = work[right]
                after = jnp.where(
                    lane < size, block, jnp.where(lane < 2 * size, 0.0, pltpu.roll(block, size, 1))
                )
            stack = jnp.concatenate([zeros, before, after, zeros], axis=0)
            change = jnp.dot(own, stack, precision=HIGH, preferred_element_type=jnp.float32)
            kept = jnp.where((lane >= size) & (lane < 3 * size), 0.0, own)
            work[keep] = kept - change
        level *= 2
    eliminate(work, [0], size // 8)
    found[0] = jnp.where(lane < size, pltpu.roll(work[0], 128 - 2 * size, 1), 0.0)
    unit = jnp.where(lane == lax.broadcasted_iota(jnp.int32, (size, 128), 0), 1.0, 0.0)
    for level, picks in reversed(steps):
        for pick in picks:
            left = -found[pick - level]
            right = -found[pick + level] if pick + level < slabs else zeros
            stack = jnp.concatenate([left, right, unit, zeros], axis=0)
            found[pick] = jnp.dot(work[pick], stack, precision=HIGH, preferred_element_type=jnp.float32)
    out_ref[...] = found[:, :, : 128 - 3 * size].reshape(slabs * size, 128 - 3 * size)


def solve_rows(rows, slabs, size, chunk=16):
    shape = (slabs, size, 128)
    return pl.pallas_call(
        functools.partial(coarse_solve, slabs, size, chunk),
        out_shape=jax.ShapeDtypeStruct((slabs * size, 128 - 3 * size), jnp.float32),
        scratch_shapes=[pltpu.VMEM(shape, jnp.float32), pltpu.VMEM(shape, jnp.float32)],
        compiler_params=pltpu.CompilerParams(vmem_limit_bytes=16 * 1024 * 1024),
    )(rows.reshape(shape))


def coarse_rows(blocks, coarse_rhs, spot, count):
    width = blocks.shape[1]
    columns = jnp.arange(count, dtype=jnp.int32)

    def placed(*parts):
        panel = jnp.zeros((width, count, width), jnp.float32)
        for block, offset in parts:
            select = (columns == spot + offset).astype(jnp.float32)
            panel = panel + block[:, None, :] * select[None, :, None]
        return panel.reshape(width, count * width)

    return jnp.concatenate(
        [
            placed((blocks[0], 0), (blocks[3], -1), (blocks[4], 1)),
            placed((blocks[1], 0)),
            placed((blocks[2], 0)),
            coarse_rhs,
        ],
        axis=1,
    )


def sweep_rows(modulus, rows):
    lane = lax.broadcasted_iota(jnp.int32, (10, 128), 1)
    spot = lax.broadcasted_iota(jnp.int32, (10, 128), 0)
    for x in range(10):
        centre = modulus[x + 1, 1:11, :]
        west = 0.5 * (centre + modulus[x, 1:11, :])
        east = 0.5 * (centre + modulus[x + 2, 1:11, :])
        south = 0.5 * (centre + modulus[x + 1, 0:10, :])
        north = 0.5 * (centre + modulus[x + 1, 2:12, :])
        lower = 0.5 * (centre + jnp.where(lane == 0, 0.0, pltpu.roll(centre, 1, 1)))
        upper = 0.5 * (centre + jnp.where(lane == 127, 0.0, pltpu.roll(centre, 127, 1)))
        diagonal = 0.002 + west + east + south + north + lower + upper
        active = centre > 0
        if x in (0, 9):
            active = active & (spot > 0) & (spot < 9)
        scale = jnp.where(active, 0.8 / diagonal, 0.0)
        rows[0, x, 0:10, :] = west * scale
        rows[1, x, 0:10, :] = east * scale
        rows[2, x, 0:10, :] = south * scale
        rows[3, x, 0:10, :] = north * scale
        rows[4, x, 0:10, :] = jnp.where(lane == 0, 0.0, lower * scale)
        rows[5, x, 0:10, :] = jnp.where(lane == 127, 0.0, upper * scale)
        rows[6, x, 0:10, :] = scale


def local_stage(
    place, found, res, vec, own_mod, west, east, south, north, out, modulus, rows, coeff, first, second, scaled
):
    modulus[2:10, 2:10, :] = own_mod[...]
    modulus[0:2, 2:10, :] = west[384:400, :].reshape(2, 8, 128)
    modulus[10:12, 2:10, :] = east[384:400, :].reshape(2, 8, 128)
    for x in range(12):
        modulus[x, 0:2, :] = south[576 + 2 * x : 578 + 2 * x, :]
        modulus[x, 10:12, :] = north[576 + 2 * x : 578 + 2 * x, :]
    sweep_rows(modulus, rows)

    parts = []
    for step_x in range(3):
        for step_y in range(3):
            start = pl.multiple_of(place[step_x * 3 + step_y], 8)
            parts.append(found[pl.ds(start, 8), :])
    near = jnp.concatenate(parts, axis=0)
    near = jnp.concatenate([near, jnp.zeros((72, 96), jnp.float32)], axis=1)
    near = jnp.concatenate([near, jnp.zeros((56, 128), jnp.float32)], axis=0)
    turned = near.T[:32]
    for index in range(72):
        coeff[index] = jnp.broadcast_to(turned[:, index : index + 1], (32, 128))

    def correct(near_index, cell, source, row_of, frozen):
        for comp in range(3):
            total = None
            for k in range(8):
                term = coeff[near_index * 8 + k] * source[pl.ds(row_of(k, comp), 1), :]
                total = term if total is None else total + term
            first[cell, comp * 32 : comp * 32 + 32, :] = total
            if frozen:
                second[cell, comp * 32 : comp * 32 + 32, :] = total

    def own_cell(index, carry):
        x, y = index // 8, index % 8
        correct(4, (x + 2) * 12 + y + 2, vec, lambda k, c: (k * 3 + c) * 64 + index, False)
        return carry

    lax.fori_loop(0, 64, own_cell, 0)

    def edge_cells(y, carry):
        for layer in range(2):
            correct(1, layer * 12 + y + 2, west, lambda k, c: ((k * 3 + c) * 2 + layer) * 8 + y, layer == 0)
            correct(7, (10 + layer) * 12 + y + 2, east, lambda k, c: ((k * 3 + c) * 2 + layer) * 8 + y, layer == 1)
            correct(3, (y + 2) * 12 + layer, south, lambda k, c: ((k * 3 + c) * 12 + y + 2) * 2 + layer, layer == 0)
            correct(5, (y + 2) * 12 + 10 + layer, north, lambda k, c: ((k * 3 + c) * 12 + y + 2) * 2 + layer, layer == 1)
        return carry

    lax.fori_loop(0, 8, edge_cells, 0)
    for x, near_x in ((1, 0), (10, 6)):
        correct(near_x, x * 12 + 1, south, lambda k, c: ((k * 3 + c) * 12 + x) * 2 + 1, True)
        correct(near_x + 2, x * 12 + 10, north, lambda k, c: ((k * 3 + c) * 12 + x) * 2, True)

    def scale_cell(x, y, source, start, stride):
        weight = rows[6, x, pl.ds(y, 1), :]
        for comp in range(3):
            scaled[x * 10 + y, comp * 32 : comp * 32 + 32, :] = (
                source[pl.ds(start(comp), 32, stride=stride), :] * weight
            )

    def own_scaled(index, carry):
        x, y = index // 8, index % 8
        scale_cell(x + 1, y + 1, res, lambda c: c * 64 + index, 192)
        return carry

    lax.fori_loop(0, 64, own_scaled, 0)

    def edge_scaled(y, carry):
        scale_cell(0, y + 1, west, lambda c: 400 + c * 8 + y, 24)
        scale_cell(9, y + 1, east, lambda c: 400 + c * 8 + y, 24)
        scale_cell(y + 1, 0, south, lambda c: 600 + c * 8 + y, 24)
        scale_cell(y + 1, 9, north, lambda c: 600 + c * 8 + y, 24)
        return carry

    lax.fori_loop(0, 8, edge_scaled, 0)

    def relax(x, y, source, store):
        cell = (x + 1) * 12 + y + 1
        weight = [rows[i, x, pl.ds(y, 1), :] for i in range(6)]
        for comp in range(3):
            span = slice(comp * 32, comp * 32 + 32)
            here = source[cell, span, :]
            value = 0.2 * here + scaled[x * 10 + y, span, :]
            value = value + weight[0] * source[cell - 12, span, :] + weight[1] * source[cell + 12, span, :]
            value = value + weight[2] * source[cell - 1, span, :] + weight[3] * source[cell + 1, span, :]
            value = value + weight[4] * pltpu.roll(here, 1, 1) + weight[5] * pltpu.roll(here, 127, 1)
            store(comp, span, value)

    for source, target in ((first, second), (second, first), (first, second)):

        def sweep(x, y, source=source, target=target):
            def keep(comp, span, value):
                target[(x + 1) * 12 + y + 1, span, :] = value

            relax(x, y, source, keep)

        def inner(index, carry, sweep=sweep):
            sweep(index // 10 + 1, index % 10)
            return carry

        def outer(y, carry, sweep=sweep):
            sweep(0, y)
            sweep(9, y)
            return carry

        lax.fori_loop(0, 80, inner, 0)
        lax.fori_loop(1, 9, outer, 0)

    def last(index, carry):
        def keep(comp, span, value):
            out[pl.ds(comp * 64 + index, 32, stride=192), :] = value

        relax(index // 8 + 1, index % 8 + 1, second, keep)
        return carry

    lax.fori_loop(0, 64, last, 0)


def local_parts(place, found, residuals, vectors, modulus, west, east, south, north):
    whole = pl.BlockSpec(memory_space=pltpu.VMEM)
    result = pl.pallas_call(
        local_stage,
        out_shape=jax.ShapeDtypeStruct((6144, 128), jnp.float32),
        in_specs=[pl.BlockSpec(memory_space=pltpu.SMEM)] + [whole] * 8,
        out_specs=whole,
        scratch_shapes=[
            pltpu.VMEM((12, 16, 128), jnp.float32),
            pltpu.VMEM((7, 10, 16, 128), jnp.float32),
            pltpu.VMEM((72, 32, 128), jnp.float32),
            pltpu.VMEM((144, 96, 128), jnp.float32),
            pltpu.VMEM((144, 96, 128), jnp.float32),
            pltpu.VMEM((100, 96, 128), jnp.float32),
        ],
        compiler_params=pltpu.CompilerParams(vmem_limit_bytes=48 * 1024 * 1024),
    )(
        place,
        found,
        residuals.reshape(6144, 128),
        vectors.reshape(1536, 128),
        modulus,
        west,
        east,
        south,
        north,
    )
    return result.reshape(residuals.shape)


def shifted(values, axis, step):
    count = lax.axis_size(axis)
    return lax.ppermute(values, axis, [(i, i + step) for i in range(count) if 0 <= i + step < count])


def lines(*arrays):
    return jnp.concatenate([array.reshape(-1, 128) for array in arrays], axis=0)


def on_device(residuals, vectors, phases, stiffness):
    count_x = lax.axis_size("gx")
    count_y = lax.axis_size("yz")
    count = count_x * count_y
    index_x = lax.axis_index("gx")
    index_y = lax.axis_index("yz")
    width = vectors.shape[0]
    levels = stiffness.shape[0]
    choose = (phases[None] == jnp.arange(levels, dtype=jnp.int32)[:, None, None, None]).astype(
        jnp.float32
    )
    modulus = jnp.sum(stiffness[:, None, None, None] * choose, axis=0)
    west = shifted(lines(vectors[:, :, 6:8], modulus[6:8], residuals[:, :, 7]), "gx", 1)
    east = shifted(lines(vectors[:, :, 0:2], modulus[0:2], residuals[:, :, 0]), "gx", -1)
    wide_vectors = jnp.concatenate(
        [west[:384].reshape(8, 3, 2, 8, 128), vectors, east[:384].reshape(8, 3, 2, 8, 128)], axis=2
    )
    wide_modulus = jnp.concatenate(
        [west[384:400].reshape(2, 8, 128), modulus, east[384:400].reshape(2, 8, 128)], axis=0
    )
    south = shifted(lines(wide_vectors[:, :, :, 6:8], wide_modulus[:, 6:8], residuals[:, :, :, 7]), "yz", 1)
    north = shifted(lines(wide_vectors[:, :, :, 0:2], wide_modulus[:, 0:2], residuals[:, :, :, 0]), "yz", -1)
    vectors_ext = jnp.concatenate(
        [south[:576].reshape(8, 3, 12, 2, 128), wide_vectors, north[:576].reshape(8, 3, 12, 2, 128)], axis=3
    )
    modulus_ext = jnp.concatenate(
        [south[576:600].reshape(12, 2, 128), wide_modulus, north[576:600].reshape(12, 2, 128)], axis=1
    )
    blocks = coarse_blocks(vectors_ext, modulus_ext)
    coarse_rhs = jnp.einsum("kcxyz,rcxyz->kr", vectors, residuals, precision=HIGH)
    own_rows = coarse_rows(blocks, coarse_rhs, index_y, count_y)
    every = jnp.broadcast_to(own_rows[None], (count,) + own_rows.shape)
    rows = lax.all_to_all(every, ("gx", "yz"), 0, 0)
    coeffs_all = solve_rows(rows, count_x, count_y * width)
    coeffs = lax.dynamic_slice_in_dim(coeffs_all, (index_x * count_y + index_y) * width, width, 0)
    near_x = jnp.clip(index_x + jnp.arange(-1, 2), 0, count_x - 1)
    near_y = jnp.clip(index_y + jnp.arange(-1, 2), 0, count_y - 1)
    place = ((near_x[:, None] * count_y + near_y[None, :]) * width).reshape(9).astype(jnp.int32)
    result = local_parts(place, coeffs_all, residuals, vectors, modulus, west, east, south, north)
    return (coeffs, result)


def solution(mesh):
    return jax.shard_map(
        on_device,
        mesh=mesh,
        in_specs=(
            P(None, None, "gx", "yz", None),
            P(None, None, "gx", "yz", None),
            P("gx", "yz", None),
            P(),
        ),
        out_specs=(P(("gx", "yz"), None), P(None, None, "gx", "yz", None)),
        check_vma=False,
    )
```

```python
import functools
import jax
import jax.numpy as jnp
from jax import lax
from jax.experimental import pallas as pl
from jax.experimental.pallas import tpu as pltpu
from jax.sharding import PartitionSpec as P

HIGH = lax.Precision.HIGHEST
GROUP = 5


def spread(values, column):
    return jnp.broadcast_to(values[:, column : column + 1], values.shape)


def fill(values, row):
    return jnp.broadcast_to(values[row : row + 1, :], values.shape)


def eliminate(work, picks, groups):
    row_index = lax.broadcasted_iota(jnp.int32, (8, 128), 0)

    def turn(step, carry):
        mats = [[work[pick, 8 * i : 8 * i + 8, :] for i in range(groups)] for pick in picks]
        for j in (0, 4):
            for mat in mats:
                cols = [[spread(mat[i], j + q) for q in range(4)] for i in range(groups)]
                r0, r1, r2, r3 = [fill(mat[0], j + q) for q in range(4)]
                p = [[fill(cols[0][q], j + i) for q in range(i + 1)] for i in range(4)]
                inverse = 1.0 / (p[0][0] * p[1][1] - p[1][0] * p[1][0])
                a0, a1, a2 = p[1][1] * inverse, -p[1][0] * inverse, p[0][0] * inverse
                y00 = p[2][0] * a0 + p[2][1] * a1
                y01 = p[2][0] * a1 + p[2][1] * a2
                y10 = p[3][0] * a0 + p[3][1] * a1
                y11 = p[3][0] * a1 + p[3][1] * a2
                s0 = p[2][2] - (y00 * p[2][0] + y01 * p[2][1])
                s1 = p[3][2] - (y10 * p[2][0] + y11 * p[2][1])
                s2 = p[3][3] - (y10 * p[3][0] + y11 * p[3][1])
                inverse = 1.0 / (s0 * s2 - s1 * s1)
                t2 = r2 - (y00 * r0 + y01 * r1)
                t3 = r3 - (y10 * r0 + y11 * r1)
                n2 = (s2 * t2 - s1 * t3) * inverse
                n3 = (s0 * t3 - s1 * t2) * inverse
                u0 = r0 - (p[2][0] * n2 + p[3][0] * n3)
                u1 = r1 - (p[2][1] * n2 + p[3][1] * n3)
                n0 = a0 * u0 + a1 * u1
                n1 = a1 * u0 + a2 * u1
                for i in range(groups):
                    changed = mat[i] - ((cols[i][0] * n0 + cols[i][1] * n1) + (cols[i][2] * n2 + cols[i][3] * n3))
                    if i == 0:
                        for q, new in enumerate((n0, n1, n2, n3)):
                            changed = jnp.where(row_index == j + q, new, changed)
                    mat[i] = changed
        for pick, mat in zip(picks, mats):
            for i in range(groups):
                to = (i + groups - 1) % groups
                work[pick, 8 * to : 8 * to + 8, :] = pltpu.roll(mat[i], 120, 1)
        return carry

    lax.fori_loop(0, groups, turn, 0)


def assemble(slabs, groups, rows_ref, work):
    lane = lax.broadcasted_iota(jnp.int32, (8, 128), 1)

    def within(start, width):
        return (lane >= start) & (lane < start + width)

    def slab(g, first):
        for h in range(groups):
            block = rows_ref[g * groups + h]
            mine = within(8 * h, min(16, 32 - 8 * h)) | within(64 + 8 * h, 8) | (lane >= 96)
            total = jnp.where(mine, block, 0.0)
            if h > 0:
                below = rows_ref[g * groups + h - 1]
                moved = pltpu.roll(below, 56, 1)
                extra = moved if h < 3 else pltpu.roll(below, 88, 1)
                total = total + jnp.where(within(8 * h - 8, 8), moved, jnp.where(within(8 * h, 8), extra, 0.0))
            if not first:
                before = rows_ref[(g - 1) * groups + h]
                moved = pltpu.roll(before, 88 if h < 3 else 120, 1)
                total = total + jnp.where(
                    within(8 * h, 8), moved, jnp.where(within(32 + 8 * h, 8), before, 0.0)
                )
            work[g, 8 * h : 8 * h + 8, :] = total

    slab(0, True)

    def later(g, carry):
        slab(g, False)
        return carry

    lax.fori_loop(1, slabs, later, 0)


def coarse_solve(slabs, size, chunk, rows_ref, out_ref, work, found):
    assemble(slabs, size // 8, rows_ref, work)
    lane = lax.broadcasted_iota(jnp.int32, (size, 128), 1)
    zeros = jnp.zeros((size, 128), jnp.float32)
    level = 1
    steps = []
    while level < slabs:
        picks = list(range(level, slabs, 2 * level))
        steps.append((level, picks))
        for at in range(0, len(picks), chunk):
            eliminate(work, picks[at : at + chunk], size // 8)
        for keep in range(0, slabs, 2 * level):
            own = work[keep]
            left, right = keep - level, keep + level
            before, after = zeros, zeros
            if left >= 0:
                block = work[left]
                before = jnp.where(
                    lane < size,
                    pltpu.roll(block, 128 - size, 1),
                    jnp.where((lane >= 2 * size) & (lane < 3 * size), 0.0, pltpu.roll(block, size, 1)),
                )
            if right < slabs:
                block = work[right]
                after = jnp.where(
                    lane < size, block, jnp.where(lane < 2 * size, 0.0, pltpu.roll(block, size, 1))
                )
            stack = jnp.concatenate([zeros, before, after, zeros], axis=0)
            change = jnp.dot(own, stack, precision=HIGH, preferred_element_type=jnp.float32)
            kept = jnp.where((lane >= size) & (lane < 3 * size), 0.0, own)
            work[keep] = kept - change
        level *= 2
    eliminate(work, [0], size // 8)
    found[0] = jnp.where(lane < size, pltpu.roll(work[0], 128 - 2 * size, 1), 0.0)
    unit = jnp.where(lane == lax.broadcasted_iota(jnp.int32, (size, 128), 0), 1.0, 0.0)
    for level, picks in reversed(steps):
        for pick in picks:
            left = -found[pick - level]
            right = -found[pick + level] if pick + level < slabs else zeros
            stack = jnp.concatenate([left, right, unit, zeros], axis=0)
            found[pick] = jnp.dot(work[pick], stack, precision=HIGH, preferred_element_type=jnp.float32)
    out_ref[...] = found[:, :, : 128 - 3 * size].reshape(slabs * size, 128 - 3 * size)


def solve_rows(rows, slabs, size, chunk=16):
    shape = (slabs, size, 128)
    return pl.pallas_call(
        functools.partial(coarse_solve, slabs, size, chunk),
        out_shape=jax.ShapeDtypeStruct((slabs * size, 128 - 3 * size), jnp.float32),
        scratch_shapes=[pltpu.VMEM(shape, jnp.float32), pltpu.VMEM(shape, jnp.float32)],
        compiler_params=pltpu.CompilerParams(vmem_limit_bytes=16 * 1024 * 1024),
        cost_estimate=pl.CostEstimate(flops=20_000_000_000, bytes_accessed=90_000_000, transcendentals=0),
    )(rows)


def lane_sums(stack):
    ones = jnp.ones((8, 128), jnp.float32)
    return lax.dot_general(
        ones, stack, (((1,), (1,)), ((), ())), precision=HIGH, preferred_element_type=jnp.float32
    )


def panel_of(parts):
    row = lax.broadcasted_iota(jnp.int32, (8, 128), 0)
    panel = jnp.zeros((8, 128), jnp.float32)
    for k in range(8):
        panel = jnp.where(row == k, lane_sums(jnp.concatenate(parts(k), axis=0)), panel)
    return panel


def project(vec, res, out):
    def cell(index, totals):
        block = res[pl.ds(index, 32, stride=192), :]
        return tuple(totals[k] + block * vec[pl.ds(k * 192 + index, 1), :] for k in range(8))

    totals = lax.fori_loop(0, 192, cell, tuple(jnp.zeros((32, 128), jnp.float32) for _ in range(8)))
    blank = jnp.zeros((96, 128), jnp.float32)
    out[...] = panel_of(lambda k: [blank, totals[k]])


def coarse_panel(spot, vec, modulus, east, north, known, out, rows, turned):
    lane = lax.broadcasted_iota(jnp.int32, (8, 128), 1)
    place = lax.broadcasted_iota(jnp.int32, (8, 128), 0)
    for x in range(8):
        centre = modulus[x]
        half = 0.5 * centre
        west = 0.5 * (centre + modulus[x - 1]) if x > 0 else half
        east_row = modulus[x + 1] if x < 7 else east[192:200, :]
        east_side = 0.5 * (centre + east_row)
        south = 0.5 * (centre + jnp.where(place == 0, 0.0, pltpu.roll(centre, 1, 0)))
        beyond = jnp.broadcast_to(north[192 + x : 193 + x, :], (8, 128))
        north_side = 0.5 * (centre + jnp.where(place == 7, beyond, pltpu.roll(centre, 7, 0)))
        lower = 0.5 * (centre + jnp.where(lane == 0, 0.0, pltpu.roll(centre, 1, 1)))
        upper = 0.5 * (centre + jnp.where(lane == 127, 0.0, pltpu.roll(centre, 127, 1)))
        span = slice(8 * x, 8 * x + 8)
        rows[0, span, :] = west if x > 0 else jnp.zeros((8, 128), jnp.float32)
        rows[1, span, :] = east_side if x < 7 else jnp.zeros((8, 128), jnp.float32)
        rows[2, span, :] = jnp.where(place == 0, 0.0, south)
        rows[3, span, :] = jnp.where(place == 7, 0.0, north_side)
        rows[4, span, :] = jnp.where(lane == 0, 0.0, lower)
        rows[5, span, :] = jnp.where(lane == 127, 0.0, upper)
        rows[6, span, :] = 0.002 + west + east_side + south + north_side + lower + upper
        rows[7, span, :] = east_side
        rows[8, span, :] = north_side

    def gather(index, carry):
        turned[index] = vec[pl.ds(index, 8, stride=192), :]
        return carry

    lax.fori_loop(0, 192, gather, 0, unroll=4)

    def own(index):
        return turned[index]

    zero = jnp.zeros((8, 128), jnp.float32)

    def cell(index, totals):
        at = index % 64
        weight = [rows[i, pl.ds(at, 1), :] for i in range(7)]
        here = own(index)
        applied = weight[6] * here - weight[4] * pltpu.roll(here, 1, 1) - weight[5] * pltpu.roll(here, 127, 1)
        applied = applied - weight[0] * own(jnp.maximum(index - 8, 0))
        applied = applied - weight[1] * own(jnp.minimum(index + 8, 191))
        applied = applied - weight[2] * own(jnp.maximum(index - 1, 0))
        applied = applied - weight[3] * own(jnp.minimum(index + 1, 191))
        return tuple(totals[k] + applied * vec[pl.ds(k * 192 + index, 1), :] for k in range(8))

    inside = lax.fori_loop(0, 192, cell, (zero,) * 8, unroll=2)

    def face(source, first, step, side):
        def spot_of(index, totals):
            comp, at = index // 8, index % 8
            cell_row = first + at * step
            mine = comp * 64 + cell_row
            weight = rows[side, pl.ds(cell_row, 1), :]
            half = 0.5 * modulus[cell_row // 8, pl.ds(cell_row % 8, 1), :]
            here = own(mine)
            there = source[pl.ds(index, 8, stride=24), :]
            toward, back, extra = -weight * there, -weight * here, half * there
            new = []
            for k in range(8):
                here_k = vec[pl.ds(k * 192 + mine, 1), :]
                there_k = source[pl.ds(k * 24 + index, 1), :]
                new += [
                    totals[3 * k] + toward * here_k,
                    totals[3 * k + 1] + back * there_k,
                    totals[3 * k + 2] + extra * there_k,
                ]
            return tuple(new)

        return lax.fori_loop(0, 24, spot_of, (zero,) * 24)

    easts = face(east, 56, 1, 7)
    norths = face(north, 7, 8, 8)

    def parts(k):
        return [
            inside[k], norths[3 * k], zero, zero,
            easts[3 * k + 1], easts[3 * k + 2], zero, zero,
            easts[3 * k], norths[3 * k + 1], norths[3 * k + 2], zero,
            zero, zero, zero, zero,
        ]

    panel = panel_of(parts)
    placed = panel
    for h in range(1, 4):
        ahead = pltpu.roll(panel, 8 * h, 1)
        behind = pltpu.roll(panel, 128 + 8 * h - 32, 1)
        moved = jnp.where(lane % 32 >= 8 * h, ahead, behind)
        placed = jnp.where(spot[0] == h, moved, placed)
    out[...] = jnp.broadcast_to((placed + known[...])[None], out.shape)


def coarse_rows(spot, residuals, vectors, modulus, east, north, count):
    whole = pl.BlockSpec(memory_space=pltpu.VMEM)
    vec = vectors.reshape(1536, 128)
    known = pl.pallas_call(
        project,
        out_shape=jax.ShapeDtypeStruct((8, 128), jnp.float32),
        in_specs=[whole, whole],
        out_specs=whole,
        compiler_params=pltpu.CompilerParams(vmem_limit_bytes=16 * 1024 * 1024),
        cost_estimate=pl.CostEstimate(flops=12_600_000, bytes_accessed=4_000_000, transcendentals=0),
    )(vec, residuals.reshape(6144, 128))
    return pl.pallas_call(
        coarse_panel,
        out_shape=jax.ShapeDtypeStruct((count, 8, 128), jnp.float32),
        in_specs=[pl.BlockSpec(memory_space=pltpu.SMEM)] + [whole] * 5,
        out_specs=whole,
        scratch_shapes=[pltpu.VMEM((9, 64, 128), jnp.float32), pltpu.VMEM((192, 8, 128), jnp.float32)],
        compiler_params=pltpu.CompilerParams(vmem_limit_bytes=16 * 1024 * 1024),
        cost_estimate=pl.CostEstimate(flops=6_000_000, bytes_accessed=2_000_000, transcendentals=0),
    )(spot, vec, modulus, east, north, known)


def sweep_rows(modulus, rows):
    lane = lax.broadcasted_iota(jnp.int32, (10, 128), 1)
    spot = lax.broadcasted_iota(jnp.int32, (10, 128), 0)
    for x in range(10):
        centre = modulus[x + 1, 1:11, :]
        west = 0.5 * (centre + modulus[x, 1:11, :])
        east = 0.5 * (centre + modulus[x + 2, 1:11, :])
        south = 0.5 * (centre + modulus[x + 1, 0:10, :])
        north = 0.5 * (centre + modulus[x + 1, 2:12, :])
        lower = 0.5 * (centre + jnp.where(lane == 0, 0.0, pltpu.roll(centre, 1, 1)))
        upper = 0.5 * (centre + jnp.where(lane == 127, 0.0, pltpu.roll(centre, 127, 1)))
        diagonal = 0.002 + west + east + south + north + lower + upper
        active = centre > 0
        if x in (0, 9):
            active = active & (spot > 0) & (spot < 9)
        scale = jnp.where(active, 0.8 / diagonal, 0.0)
        rows[0, x, 0:10, :] = west * scale
        rows[1, x, 0:10, :] = east * scale
        rows[2, x, 0:10, :] = south * scale
        rows[3, x, 0:10, :] = north * scale
        rows[4, x, 0:10, :] = jnp.where(lane == 0, 0.0, lower * scale)
        rows[5, x, 0:10, :] = jnp.where(lane == 127, 0.0, upper * scale)
        rows[6, x, 0:10, :] = scale


def local_stage(
    place, found, res, vec, own_mod, west, east, south, north, out, modulus, rows, coeff, first, second, scaled, shift
):
    modulus[2:10, 2:10, :] = own_mod[...]
    modulus[0:2, 2:10, :] = west[384:400, :].reshape(2, 8, 128)
    modulus[10:12, 2:10, :] = east[384:400, :].reshape(2, 8, 128)
    for x in range(12):
        modulus[x, 0:2, :] = south[576 + 2 * x : 578 + 2 * x, :]
        modulus[x, 10:12, :] = north[576 + 2 * x : 578 + 2 * x, :]
    sweep_rows(modulus, rows)

    parts = []
    for step_x in range(3):
        for step_y in range(3):
            start = pl.multiple_of(place[step_x * 3 + step_y], 8)
            parts.append(found[pl.ds(start, 8), :])
    near = jnp.concatenate(parts, axis=0)
    near = jnp.concatenate([near, jnp.zeros((72, 96), jnp.float32)], axis=1)
    near = jnp.concatenate([near, jnp.zeros((56, 128), jnp.float32)], axis=0)
    turned = near.T[:32]
    for index in range(72):
        coeff[index] = jnp.broadcast_to(turned[:, index : index + 1], (32, 128))

    def correct(near_index, cell, source, row_of, frozen):
        for comp in range(3):
            total = None
            for k in range(8):
                term = coeff[near_index * 8 + k] * source[pl.ds(row_of(k, comp), 1), :]
                total = term if total is None else total + term
            first[cell, comp * 32 : comp * 32 + 32, :] = total
            if frozen:
                second[cell, comp * 32 : comp * 32 + 32, :] = total

    def own_cell(index, carry):
        x, y = index // 8, index % 8
        correct(4, (x + 2) * 12 + y + 2, vec, lambda k, c: (k * 3 + c) * 64 + index, False)
        return carry

    lax.fori_loop(0, 64, own_cell, 0)

    def edge_cells(y, carry):
        for layer in range(2):
            correct(1, layer * 12 + y + 2, west, lambda k, c: ((k * 3 + c) * 2 + layer) * 8 + y, layer == 0)
            correct(7, (10 + layer) * 12 + y + 2, east, lambda k, c: ((k * 3 + c) * 2 + layer) * 8 + y, layer == 1)
            correct(3, (y + 2) * 12 + layer, south, lambda k, c: ((k * 3 + c) * 12 + y + 2) * 2 + layer, layer == 0)
            correct(5, (y + 2) * 12 + 10 + layer, north, lambda k, c: ((k * 3 + c) * 12 + y + 2) * 2 + layer, layer == 1)
        return carry

    lax.fori_loop(0, 8, edge_cells, 0)
    for x, near_x in ((1, 0), (10, 6)):
        correct(near_x, x * 12 + 1, south, lambda k, c: ((k * 3 + c) * 12 + x) * 2 + 1, True)
        correct(near_x + 2, x * 12 + 10, north, lambda k, c: ((k * 3 + c) * 12 + x) * 2, True)

    def scale_cell(x, y, source, start, stride):
        weight = rows[6, x, pl.ds(y, 1), :]
        for comp in range(3):
            scaled[x * 10 + y, comp * 32 : comp * 32 + 32, :] = (
                source[pl.ds(start(comp), 32, stride=stride), :] * weight
            )

    def own_scaled(index, carry):
        x, y = index // 8, index % 8
        scale_cell(x + 1, y + 1, res, lambda c: c * 64 + index, 192)
        return carry

    lax.fori_loop(0, 64, own_scaled, 0)

    def edge_scaled(y, carry):
        scale_cell(0, y + 1, west, lambda c: 400 + c * 8 + y, 24)
        scale_cell(9, y + 1, east, lambda c: 400 + c * 8 + y, 24)
        scale_cell(y + 1, 0, south, lambda c: 600 + c * 8 + y, 24)
        scale_cell(y + 1, 9, north, lambda c: 600 + c * 8 + y, 24)
        return carry

    lax.fori_loop(0, 8, edge_scaled, 0)

    up = lax.broadcasted_iota(jnp.int32, (256, 256), 0) % 128
    to = lax.broadcasted_iota(jnp.int32, (256, 256), 1)
    moves = ((to < 128) & (to == up + 1)) | ((to >= 128) & (to - 128 == up - 1))
    shift[...] = jnp.where(moves, 1.0, 0.0).astype(jnp.bfloat16)

    def relax(x, y, cells, source, store):
        cell = (x + 1) * 12 + y + 1
        block = source[pl.ds(cell, cells)].reshape(cells * 96, 128)
        high = block.astype(jnp.bfloat16)
        rest = (block - high.astype(jnp.float32)).astype(jnp.bfloat16)
        moved = jnp.dot(
            jnp.concatenate([high, rest], axis=1), shift[...], preferred_element_type=jnp.float32
        )
        for n in range(cells):
            weight = [rows[i, x, pl.ds(y + n, 1), :] for i in range(6)]
            here = moved[n * 96 : n * 96 + 96]
            value = 0.2 * source[cell + n] + scaled[x * 10 + y + n]
            value = value + weight[0] * source[cell + n - 12] + weight[1] * source[cell + n + 12]
            value = value + weight[2] * source[cell + n - 1] + weight[3] * source[cell + n + 1]
            value = value + weight[4] * here[:, :128] + weight[5] * here[:, 128:]
            store(n, value)

    for source, target in ((first, second), (second, first), (first, second)):

        def sweep(x, y, cells, source=source, target=target):
            def keep(n, value):
                target[(x + 1) * 12 + y + n + 1] = value

            relax(x, y, cells, source, keep)

        def inner(index, carry, sweep=sweep):
            for y in range(0, 10, GROUP):
                sweep(index + 1, y, GROUP)
            return carry

        lax.fori_loop(0, 8, inner, 0)
        for x in (0, 9):
            for y in range(1, 9, 4):
                sweep(x, y, 4)

    def last(x, carry):
        for y in range(0, 8, 4):

            def keep(n, value, y=y):
                for comp in range(3):
                    out[pl.ds(comp * 64 + x * 8 + y + n, 32, stride=192), :] = value[comp * 32 : comp * 32 + 32]

            relax(x + 1, y + 1, 4, second, keep)
        return carry

    lax.fori_loop(0, 8, last, 0)


def local_parts(place, found, residuals, vectors, modulus, west, east, south, north):
    whole = pl.BlockSpec(memory_space=pltpu.VMEM)
    result = pl.pallas_call(
        local_stage,
        out_shape=jax.ShapeDtypeStruct((6144, 128), jnp.float32),
        in_specs=[pl.BlockSpec(memory_space=pltpu.SMEM)] + [whole] * 8,
        out_specs=whole,
        scratch_shapes=[
            pltpu.VMEM((12, 16, 128), jnp.float32),
            pltpu.VMEM((7, 10, 16, 128), jnp.float32),
            pltpu.VMEM((72, 32, 128), jnp.float32),
            pltpu.VMEM((144, 96, 128), jnp.float32),
            pltpu.VMEM((144, 96, 128), jnp.float32),
            pltpu.VMEM((100, 96, 128), jnp.float32),
            pltpu.VMEM((256, 256), jnp.bfloat16),
        ],
        compiler_params=pltpu.CompilerParams(vmem_limit_bytes=48 * 1024 * 1024),
    )(
        place,
        found,
        residuals.reshape(6144, 128),
        vectors.reshape(1536, 128),
        modulus,
        west,
        east,
        south,
        north,
    )
    return result.reshape(residuals.shape)

def shifted(values, axis, step):
    count = lax.axis_size(axis)
    return lax.ppermute(values, axis, [(i, i + step) for i in range(count) if 0 <= i + step < count])


def lines(*arrays):
    return jnp.concatenate([array.reshape(-1, 128) for array in arrays], axis=0)


def on_device(residuals, vectors, phases, stiffness):
    count_x = lax.axis_size("gx")
    count_y = lax.axis_size("yz")
    count = count_x * count_y
    index_x = lax.axis_index("gx")
    index_y = lax.axis_index("yz")
    width = vectors.shape[0]
    levels = stiffness.shape[0]
    choose = (phases[None] == jnp.arange(levels, dtype=jnp.int32)[:, None, None, None]).astype(
        jnp.float32
    )
    modulus = jnp.sum(stiffness[:, None, None, None] * choose, axis=0)
    east_face = shifted(lines(vectors[:, :, 0], modulus[0]), "gx", -1)
    north_face = shifted(lines(vectors[:, :, :, 0], modulus[:, 0]), "yz", -1)
    spot = index_y.astype(jnp.int32).reshape(1)
    every = coarse_rows(spot, residuals, vectors, modulus, east_face, north_face, count)
    to_west = lines(vectors[:, :, 0:2], modulus[0:2], residuals[:, :, 0])
    to_east = lines(vectors[:, :, 6:8], modulus[6:8], residuals[:, :, 7])
    every, to_west, to_east = lax.optimization_barrier((every, to_west, to_east))
    rows = lax.all_to_all(every, ("gx", "yz"), 0, 0)
    west = shifted(to_east, "gx", 1)
    east = shifted(to_west, "gx", -1)
    wide_vectors = jnp.concatenate(
        [west[:384].reshape(8, 3, 2, 8, 128), vectors, east[:384].reshape(8, 3, 2, 8, 128)], axis=2
    )
    wide_modulus = jnp.concatenate(
        [west[384:400].reshape(2, 8, 128), modulus, east[384:400].reshape(2, 8, 128)], axis=0
    )
    south = shifted(lines(wide_vectors[:, :, :, 6:8], wide_modulus[:, 6:8], residuals[:, :, :, 7]), "yz", 1)
    north = shifted(lines(wide_vectors[:, :, :, 0:2], wide_modulus[:, 0:2], residuals[:, :, :, 0]), "yz", -1)
    coeffs_all = solve_rows(rows, count_x, count_y * width)
    coeffs = lax.dynamic_slice_in_dim(coeffs_all, (index_x * count_y + index_y) * width, width, 0)
    near_x = jnp.clip(index_x + jnp.arange(-1, 2), 0, count_x - 1)
    near_y = jnp.clip(index_y + jnp.arange(-1, 2), 0, count_y - 1)
    place = ((near_x[:, None] * count_y + near_y[None, :]) * width).reshape(9).astype(jnp.int32)
    result = local_parts(place, coeffs_all, residuals, vectors, modulus, west, east, south, north)
    return (coeffs, result)


def solution(mesh):
    return jax.shard_map(
        on_device,
        mesh=mesh,
        in_specs=(
            P(None, None, "gx", "yz", None),
            P(None, None, "gx", "yz", None),
            P("gx", "yz", None),
            P(),
        ),
        out_specs=(P(("gx", "yz"), None), P(None, None, "gx", "yz", None)),
        check_vma=False,
    )
```

```python
import functools
import jax
import jax.numpy as jnp
from jax import lax
from jax.experimental import pallas as pl
from jax.experimental.pallas import tpu as pltpu
from jax.sharding import PartitionSpec as P

HIGH = lax.Precision.HIGHEST
GROUP = 5


def spread(values, column):
    return jnp.broadcast_to(values[:, column : column + 1], values.shape)


def fill(values, row):
    return jnp.broadcast_to(values[row : row + 1, :], values.shape)


def eliminate(work, picks, groups):
    row_index = lax.broadcasted_iota(jnp.int32, (8, 128), 0)

    def turn(step, carry):
        mats = [[work[pick, 8 * i : 8 * i + 8, :] for i in range(groups)] for pick in picks]
        for j in (0, 4):
            for mat in mats:
                cols = [[spread(mat[i], j + q) for q in range(4)] for i in range(groups)]
                r0, r1, r2, r3 = [fill(mat[0], j + q) for q in range(4)]
                p = [[fill(cols[0][q], j + i) for q in range(i + 1)] for i in range(4)]
                inverse = 1.0 / (p[0][0] * p[1][1] - p[1][0] * p[1][0])
                a0, a1, a2 = p[1][1] * inverse, -p[1][0] * inverse, p[0][0] * inverse
                y00 = p[2][0] * a0 + p[2][1] * a1
                y01 = p[2][0] * a1 + p[2][1] * a2
                y10 = p[3][0] * a0 + p[3][1] * a1
                y11 = p[3][0] * a1 + p[3][1] * a2
                s0 = p[2][2] - (y00 * p[2][0] + y01 * p[2][1])
                s1 = p[3][2] - (y10 * p[2][0] + y11 * p[2][1])
                s2 = p[3][3] - (y10 * p[3][0] + y11 * p[3][1])
                inverse = 1.0 / (s0 * s2 - s1 * s1)
                t2 = r2 - (y00 * r0 + y01 * r1)
                t3 = r3 - (y10 * r0 + y11 * r1)
                n2 = (s2 * t2 - s1 * t3) * inverse
                n3 = (s0 * t3 - s1 * t2) * inverse
                u0 = r0 - (p[2][0] * n2 + p[3][0] * n3)
                u1 = r1 - (p[2][1] * n2 + p[3][1] * n3)
                n0 = a0 * u0 + a1 * u1
                n1 = a1 * u0 + a2 * u1
                for i in range(groups):
                    changed = mat[i] - ((cols[i][0] * n0 + cols[i][1] * n1) + (cols[i][2] * n2 + cols[i][3] * n3))
                    if i == 0:
                        for q, new in enumerate((n0, n1, n2, n3)):
                            changed = jnp.where(row_index == j + q, new, changed)
                    mat[i] = changed
        for pick, mat in zip(picks, mats):
            for i in range(groups):
                to = (i + groups - 1) % groups
                work[pick, 8 * to : 8 * to + 8, :] = pltpu.roll(mat[i], 120, 1)
        return carry

    lax.fori_loop(0, groups, turn, 0)


def assemble(slabs, groups, rows_ref, work):
    lane = lax.broadcasted_iota(jnp.int32, (8, 128), 1)

    def within(start, width):
        return (lane >= start) & (lane < start + width)

    def slab(g, first):
        for h in range(groups):
            block = rows_ref[g * groups + h]
            mine = within(8 * h, min(16, 32 - 8 * h)) | within(64 + 8 * h, 8) | (lane >= 96)
            total = jnp.where(mine, block, 0.0)
            if h > 0:
                below = rows_ref[g * groups + h - 1]
                moved = pltpu.roll(below, 56, 1)
                extra = moved if h < 3 else pltpu.roll(below, 88, 1)
                total = total + jnp.where(within(8 * h - 8, 8), moved, jnp.where(within(8 * h, 8), extra, 0.0))
            if not first:
                before = rows_ref[(g - 1) * groups + h]
                moved = pltpu.roll(before, 88 if h < 3 else 120, 1)
                total = total + jnp.where(
                    within(8 * h, 8), moved, jnp.where(within(32 + 8 * h, 8), before, 0.0)
                )
            work[g, 8 * h : 8 * h + 8, :] = total

    slab(0, True)

    def later(g, carry):
        slab(g, False)
        return carry

    lax.fori_loop(1, slabs, later, 0)


def coarse_solve(slabs, size, chunk, spot, rows_ref, own_ref, near_ref, work, found):
    assemble(slabs, size // 8, rows_ref, work)
    lane = lax.broadcasted_iota(jnp.int32, (size, 128), 1)
    zeros = jnp.zeros((size, 128), jnp.float32)
    level = 1
    steps = []
    while level < slabs:
        picks = list(range(level, slabs, 2 * level))
        steps.append((level, picks))
        for at in range(0, len(picks), chunk):
            eliminate(work, picks[at : at + chunk], size // 8)
        for keep in range(0, slabs, 2 * level):
            own = work[keep]
            left, right = keep - level, keep + level
            before, after = zeros, zeros
            if left >= 0:
                block = work[left]
                before = jnp.where(
                    lane < size,
                    pltpu.roll(block, 128 - size, 1),
                    jnp.where((lane >= 2 * size) & (lane < 3 * size), 0.0, pltpu.roll(block, size, 1)),
                )
            if right < slabs:
                block = work[right]
                after = jnp.where(
                    lane < size, block, jnp.where(lane < 2 * size, 0.0, pltpu.roll(block, size, 1))
                )
            stack = jnp.concatenate([zeros, before, after, zeros], axis=0)
            change = jnp.dot(own, stack, precision=HIGH, preferred_element_type=jnp.float32)
            kept = jnp.where((lane >= size) & (lane < 3 * size), 0.0, own)
            work[keep] = kept - change
        level *= 2
    eliminate(work, [0], size // 8)
    found[...] = jnp.zeros(found.shape, jnp.float32)
    found[0] = jnp.where(lane < size, pltpu.roll(work[0], 128 - 2 * size, 1), 0.0)
    unit = jnp.where(lane == lax.broadcasted_iota(jnp.int32, (size, 128), 0), 1.0, 0.0)
    lowest = jnp.maximum(spot[0] - 1, 0)
    for level, picks in reversed(steps):
        first = lowest // level
        first = first + 1 - first % 2
        for wanted in (first, first + 2)[: len(picks)]:
            pick = jnp.minimum(wanted, slabs // level - 1) * level
            left, right = -found[pick - level], -found[pick + level]
            stack = jnp.concatenate([left, right, unit, zeros], axis=0)
            found[pick] = jnp.dot(work[pick], stack, precision=HIGH, preferred_element_type=jnp.float32)
    width = 128 - 3 * size

    def taken(slab, row):
        return found[slab, pl.ds(pl.multiple_of(row * 8, 8), 8), :][:, :width]

    own_ref[...] = taken(spot[0], spot[1])
    for step_x in range(3):
        for step_y in range(3):
            slab = jnp.clip(spot[0] + step_x - 1, 0, slabs - 1)
            row = jnp.clip(spot[1] + step_y - 1, 0, size // 8 - 1)
            at = (step_x * 3 + step_y) * 8
            near_ref[at : at + 8, :] = taken(slab, row)


def solve_rows(spot, rows, slabs, size, chunk=16):
    width = 128 - 3 * size
    whole = pl.BlockSpec(memory_space=pltpu.VMEM)
    return pl.pallas_call(
        functools.partial(coarse_solve, slabs, size, chunk),
        out_shape=(
            jax.ShapeDtypeStruct((8, width), jnp.float32),
            jax.ShapeDtypeStruct((72, width), jnp.float32),
        ),
        in_specs=[pl.BlockSpec(memory_space=pltpu.SMEM), whole],
        out_specs=(whole, whole),
        scratch_shapes=[
            pltpu.VMEM((slabs, size, 128), jnp.float32),
            pltpu.VMEM((slabs + 1, size, 128), jnp.float32),
        ],
        compiler_params=pltpu.CompilerParams(vmem_limit_bytes=16 * 1024 * 1024),
        cost_estimate=pl.CostEstimate(flops=20_000_000_000, bytes_accessed=90_000_000, transcendentals=0),
    )(spot, rows)


def panel_of(slots):
    lane = lax.broadcasted_iota(jnp.int32, (8, 128), 1)
    stack = jnp.concatenate([part for parts in slots for part in parts], axis=0)
    ones = jnp.ones((128, 128), jnp.float32)
    sums = jnp.dot(stack, ones, precision=HIGH, preferred_element_type=jnp.float32)
    columns = []
    at = 0
    for parts in slots:
        column = jnp.zeros((8, 128), jnp.float32)
        for k in range(len(parts)):
            column = jnp.where(lane == k, sums[at : at + 8], column)
            at += 8
        columns.append(column)
    return jnp.concatenate(columns, axis=0).T[:8]


def project(vec, res, out):
    def cell(index, totals):
        block = res[pl.ds(index, 32, stride=192), :]
        return tuple(totals[k] + block * vec[pl.ds(k * 192 + index, 1), :] for k in range(8))

    totals = lax.fori_loop(0, 192, cell, tuple(jnp.zeros((32, 128), jnp.float32) for _ in range(8)), unroll=4)
    slots = [[totals[k][8 * i : 8 * i + 8] for k in range(8)] for i in range(4)]
    out[...] = panel_of([[]] * 12 + slots)


def coarse_panel(spot, vec, modulus, east, north, known, out, rows, turned):
    lane = lax.broadcasted_iota(jnp.int32, (8, 128), 1)
    place = lax.broadcasted_iota(jnp.int32, (8, 128), 0)
    for x in range(8):
        centre = modulus[x]
        half = 0.5 * centre
        west = 0.5 * (centre + modulus[x - 1]) if x > 0 else half
        east_row = modulus[x + 1] if x < 7 else east[192:200, :]
        east_side = 0.5 * (centre + east_row)
        south = 0.5 * (centre + jnp.where(place == 0, 0.0, pltpu.roll(centre, 1, 0)))
        beyond = jnp.broadcast_to(north[192 + x : 193 + x, :], (8, 128))
        north_side = 0.5 * (centre + jnp.where(place == 7, beyond, pltpu.roll(centre, 7, 0)))
        lower = 0.5 * (centre + jnp.where(lane == 0, 0.0, pltpu.roll(centre, 1, 1)))
        upper = 0.5 * (centre + jnp.where(lane == 127, 0.0, pltpu.roll(centre, 127, 1)))
        span = slice(8 * x, 8 * x + 8)
        rows[0, span, :] = west if x > 0 else jnp.zeros((8, 128), jnp.float32)
        rows[1, span, :] = east_side if x < 7 else jnp.zeros((8, 128), jnp.float32)
        rows[2, span, :] = jnp.where(place == 0, 0.0, south)
        rows[3, span, :] = jnp.where(place == 7, 0.0, north_side)
        rows[4, span, :] = jnp.where(lane == 0, 0.0, lower)
        rows[5, span, :] = jnp.where(lane == 127, 0.0, upper)
        rows[6, span, :] = 0.002 + west + east_side + south + north_side + lower + upper
        rows[7, span, :] = east_side
        rows[8, span, :] = north_side

    def gather(index, carry):
        turned[index] = vec[pl.ds(index, 8, stride=192), :]
        return carry

    lax.fori_loop(0, 192, gather, 0, unroll=4)

    def own(index):
        return turned[index]

    zero = jnp.zeros((8, 128), jnp.float32)

    def cell(index, totals):
        at = index % 64
        weight = [rows[i, pl.ds(at, 1), :] for i in range(7)]
        here = own(index)
        applied = weight[6] * here - weight[4] * pltpu.roll(here, 1, 1) - weight[5] * pltpu.roll(here, 127, 1)
        applied = applied - weight[0] * own(jnp.maximum(index - 8, 0))
        applied = applied - weight[1] * own(jnp.minimum(index + 8, 191))
        applied = applied - weight[2] * own(jnp.maximum(index - 1, 0))
        applied = applied - weight[3] * own(jnp.minimum(index + 1, 191))
        return tuple(totals[k] + applied * vec[pl.ds(k * 192 + index, 1), :] for k in range(8))

    inside = lax.fori_loop(0, 192, cell, (zero,) * 8, unroll=8)

    def face(source, first, step, side):
        def spot_of(index, totals):
            comp, at = index // 8, index % 8
            cell_row = first + at * step
            mine = comp * 64 + cell_row
            weight = rows[side, pl.ds(cell_row, 1), :]
            half = 0.5 * modulus[cell_row // 8, pl.ds(cell_row % 8, 1), :]
            here = own(mine)
            there = source[pl.ds(index, 8, stride=24), :]
            toward, back, extra = -weight * there, -weight * here, half * there
            new = []
            for k in range(8):
                here_k = vec[pl.ds(k * 192 + mine, 1), :]
                there_k = source[pl.ds(k * 24 + index, 1), :]
                new += [
                    totals[3 * k] + toward * here_k,
                    totals[3 * k + 1] + back * there_k,
                    totals[3 * k + 2] + extra * there_k,
                ]
            return tuple(new)

        return lax.fori_loop(0, 24, spot_of, (zero,) * 24)

    easts = face(east, 56, 1, 7)
    norths = face(north, 7, 8, 8)

    panel = panel_of(
        [
            inside, norths[0::3], [], [],
            easts[1::3], easts[2::3], [], [],
            easts[0::3], norths[1::3], norths[2::3], [],
            [], [], [], [],
        ]
    )
    placed = panel
    for h in range(1, 4):
        ahead = pltpu.roll(panel, 8 * h, 1)
        behind = pltpu.roll(panel, 128 + 8 * h - 32, 1)
        moved = jnp.where(lane % 32 >= 8 * h, ahead, behind)
        placed = jnp.where(spot[1] == h, moved, placed)
    out[...] = jnp.broadcast_to((placed + known[...])[None], out.shape)


def coarse_rows(spot, residuals, vectors, modulus, east, north, count):
    whole = pl.BlockSpec(memory_space=pltpu.VMEM)
    vec = vectors.reshape(1536, 128)
    known = pl.pallas_call(
        project,
        out_shape=jax.ShapeDtypeStruct((8, 128), jnp.float32),
        in_specs=[whole, whole],
        out_specs=whole,
        compiler_params=pltpu.CompilerParams(vmem_limit_bytes=16 * 1024 * 1024),
        cost_estimate=pl.CostEstimate(flops=12_600_000, bytes_accessed=4_000_000, transcendentals=0),
    )(vec, residuals.reshape(6144, 128))
    return pl.pallas_call(
        coarse_panel,
        out_shape=jax.ShapeDtypeStruct((count, 8, 128), jnp.float32),
        in_specs=[pl.BlockSpec(memory_space=pltpu.SMEM)] + [whole] * 5,
        out_specs=whole,
        scratch_shapes=[pltpu.VMEM((9, 64, 128), jnp.float32), pltpu.VMEM((192, 8, 128), jnp.float32)],
        compiler_params=pltpu.CompilerParams(vmem_limit_bytes=16 * 1024 * 1024),
        cost_estimate=pl.CostEstimate(flops=6_000_000, bytes_accessed=2_000_000, transcendentals=0),
    )(spot, vec, modulus, east, north, known)


def sweep_rows(modulus, rows):
    lane = lax.broadcasted_iota(jnp.int32, (10, 128), 1)
    spot = lax.broadcasted_iota(jnp.int32, (10, 128), 0)
    for x in range(10):
        centre = modulus[x + 1, 1:11, :]
        west = 0.5 * (centre + modulus[x, 1:11, :])
        east = 0.5 * (centre + modulus[x + 2, 1:11, :])
        south = 0.5 * (centre + modulus[x + 1, 0:10, :])
        north = 0.5 * (centre + modulus[x + 1, 2:12, :])
        lower = 0.5 * (centre + jnp.where(lane == 0, 0.0, pltpu.roll(centre, 1, 1)))
        upper = 0.5 * (centre + jnp.where(lane == 127, 0.0, pltpu.roll(centre, 127, 1)))
        diagonal = 0.002 + west + east + south + north + lower + upper
        active = centre > 0
        if x in (0, 9):
            active = active & (spot > 0) & (spot < 9)
        scale = jnp.where(active, 0.8 / diagonal, 0.0)
        rows[0, x, 0:10, :] = west * scale
        rows[1, x, 0:10, :] = east * scale
        rows[2, x, 0:10, :] = south * scale
        rows[3, x, 0:10, :] = north * scale
        rows[4, x, 0:10, :] = jnp.where(lane == 0, 0.0, lower * scale)
        rows[5, x, 0:10, :] = jnp.where(lane == 127, 0.0, upper * scale)
        rows[6, x, 0:10, :] = scale


def local_stage(
    near_ref, res, vec, own_mod, west, east, south, north, out, modulus, rows, coeff, first, second, scaled, shift
):
    modulus[2:10, 2:10, :] = own_mod[...]
    modulus[0:2, 2:10, :] = west[384:400, :].reshape(2, 8, 128)
    modulus[10:12, 2:10, :] = east[384:400, :].reshape(2, 8, 128)
    for x in range(12):
        modulus[x, 0:2, :] = south[576 + 2 * x : 578 + 2 * x, :]
        modulus[x, 10:12, :] = north[576 + 2 * x : 578 + 2 * x, :]
    sweep_rows(modulus, rows)

    near = near_ref[...]
    near = jnp.concatenate([near, jnp.zeros((72, 96), jnp.float32)], axis=1)
    near = jnp.concatenate([near, jnp.zeros((56, 128), jnp.float32)], axis=0)
    turned = near.T[:32]
    for index in range(72):
        coeff[index] = jnp.broadcast_to(turned[:, index : index + 1], (32, 128))

    def correct(near_index, cell, source, row_of, frozen):
        for comp in range(3):
            total = None
            for k in range(8):
                term = coeff[near_index * 8 + k] * source[pl.ds(row_of(k, comp), 1), :]
                total = term if total is None else total + term
            first[cell, comp * 32 : comp * 32 + 32, :] = total
            if frozen:
                second[cell, comp * 32 : comp * 32 + 32, :] = total

    def own_cell(index, carry):
        x, y = index // 8, index % 8
        correct(4, (x + 2) * 12 + y + 2, vec, lambda k, c: (k * 3 + c) * 64 + index, False)
        return carry

    lax.fori_loop(0, 64, own_cell, 0, unroll=2)

    def edge_cells(y, carry):
        for layer in range(2):
            correct(1, layer * 12 + y + 2, west, lambda k, c: ((k * 3 + c) * 2 + layer) * 8 + y, layer == 0)
            correct(7, (10 + layer) * 12 + y + 2, east, lambda k, c: ((k * 3 + c) * 2 + layer) * 8 + y, layer == 1)
            correct(3, (y + 2) * 12 + layer, south, lambda k, c: ((k * 3 + c) * 12 + y + 2) * 2 + layer, layer == 0)
            correct(5, (y + 2) * 12 + 10 + layer, north, lambda k, c: ((k * 3 + c) * 12 + y + 2) * 2 + layer, layer == 1)
        return carry

    lax.fori_loop(0, 8, edge_cells, 0)
    for x, near_x in ((1, 0), (10, 6)):
        correct(near_x, x * 12 + 1, south, lambda k, c: ((k * 3 + c) * 12 + x) * 2 + 1, True)
        correct(near_x + 2, x * 12 + 10, north, lambda k, c: ((k * 3 + c) * 12 + x) * 2, True)

    def scale_cell(x, y, source, start, stride):
        weight = rows[6, x, pl.ds(y, 1), :]
        for comp in range(3):
            scaled[x * 10 + y, comp * 32 : comp * 32 + 32, :] = (
                source[pl.ds(start(comp), 32, stride=stride), :] * weight
            )

    def own_scaled(index, carry):
        x, y = index // 8, index % 8
        scale_cell(x + 1, y + 1, res, lambda c: c * 64 + index, 192)
        return carry

    lax.fori_loop(0, 64, own_scaled, 0, unroll=4)

    def edge_scaled(y, carry):
        scale_cell(0, y + 1, west, lambda c: 400 + c * 8 + y, 24)
        scale_cell(9, y + 1, east, lambda c: 400 + c * 8 + y, 24)
        scale_cell(y + 1, 0, south, lambda c: 600 + c * 8 + y, 24)
        scale_cell(y + 1, 9, north, lambda c: 600 + c * 8 + y, 24)
        return carry

    lax.fori_loop(0, 8, edge_scaled, 0, unroll=2)

    up = lax.broadcasted_iota(jnp.int32, (256, 256), 0) % 128
    to = lax.broadcasted_iota(jnp.int32, (256, 256), 1)
    moves = ((to < 128) & (to == up + 1)) | ((to >= 128) & (to - 128 == up - 1))
    shift[...] = jnp.where(moves, 1.0, 0.0).astype(jnp.bfloat16)

    def relax(x, y, cells, source, store):
        cell = (x + 1) * 12 + y + 1
        block = source[pl.ds(cell, cells)].reshape(cells * 96, 128)
        high = block.astype(jnp.bfloat16)
        rest = (block - high.astype(jnp.float32)).astype(jnp.bfloat16)
        moved = jnp.dot(
            jnp.concatenate([high, rest], axis=1), shift[...], preferred_element_type=jnp.float32
        )
        for n in range(cells):
            weight = [rows[i, x, pl.ds(y + n, 1), :] for i in range(6)]
            here = moved[n * 96 : n * 96 + 96]
            value = 0.2 * source[cell + n] + scaled[x * 10 + y + n]
            value = value + weight[0] * source[cell + n - 12] + weight[1] * source[cell + n + 12]
            value = value + weight[2] * source[cell + n - 1] + weight[3] * source[cell + n + 1]
            value = value + weight[4] * here[:, :128] + weight[5] * here[:, 128:]
            store(n, value)

    for source, target in ((first, second), (second, first), (first, second)):

        def sweep(x, y, cells, source=source, target=target):
            def keep(n, value):
                target[(x + 1) * 12 + y + n + 1] = value

            relax(x, y, cells, source, keep)

        def inner(index, carry, sweep=sweep):
            for y in range(0, 10, GROUP):
                sweep(index + 1, y, GROUP)
            return carry

        lax.fori_loop(0, 8, inner, 0)
        for x in (0, 9):
            for y in range(1, 9, 4):
                sweep(x, y, 4)

    def last(x, carry):
        for y in range(0, 8, 4):

            def keep(n, value, y=y):
                for comp in range(3):
                    out[pl.ds(comp * 64 + x * 8 + y + n, 32, stride=192), :] = value[comp * 32 : comp * 32 + 32]

            relax(x + 1, y + 1, 4, second, keep)
        return carry

    lax.fori_loop(0, 8, last, 0)


def local_parts(near, residuals, vectors, modulus, west, east, south, north):
    whole = pl.BlockSpec(memory_space=pltpu.VMEM)
    result = pl.pallas_call(
        local_stage,
        out_shape=jax.ShapeDtypeStruct((6144, 128), jnp.float32),
        in_specs=[whole] * 8,
        out_specs=whole,
        scratch_shapes=[
            pltpu.VMEM((12, 16, 128), jnp.float32),
            pltpu.VMEM((7, 10, 16, 128), jnp.float32),
            pltpu.VMEM((72, 32, 128), jnp.float32),
            pltpu.VMEM((144, 96, 128), jnp.float32),
            pltpu.VMEM((144, 96, 128), jnp.float32),
            pltpu.VMEM((100, 96, 128), jnp.float32),
            pltpu.VMEM((256, 256), jnp.bfloat16),
        ],
        compiler_params=pltpu.CompilerParams(vmem_limit_bytes=48 * 1024 * 1024),
    )(
        near,
        residuals.reshape(6144, 128),
        vectors.reshape(1536, 128),
        modulus,
        west,
        east,
        south,
        north,
    )
    return result.reshape(residuals.shape)

def shifted(values, axis, step):
    count = lax.axis_size(axis)
    return lax.ppermute(values, axis, [(i, i + step) for i in range(count) if 0 <= i + step < count])


def lines(*arrays):
    return jnp.concatenate([array.reshape(-1, 128) for array in arrays], axis=0)


def on_device(residuals, vectors, phases, stiffness):
    count_x = lax.axis_size("gx")
    count_y = lax.axis_size("yz")
    count = count_x * count_y
    index_x = lax.axis_index("gx")
    index_y = lax.axis_index("yz")
    width = vectors.shape[0]
    levels = stiffness.shape[0]
    choose = (phases[None] == jnp.arange(levels, dtype=jnp.int32)[:, None, None, None]).astype(
        jnp.float32
    )
    modulus = jnp.sum(stiffness[:, None, None, None] * choose, axis=0)
    east_face = shifted(lines(vectors[:, :, 0], modulus[0]), "gx", -1)
    north_face = shifted(lines(vectors[:, :, :, 0], modulus[:, 0]), "yz", -1)
    spot = jnp.stack([index_x, index_y]).astype(jnp.int32)
    every = coarse_rows(spot, residuals, vectors, modulus, east_face, north_face, count)
    to_west = lines(vectors[:, :, 0:2], modulus[0:2], residuals[:, :, 0])
    to_east = lines(vectors[:, :, 6:8], modulus[6:8], residuals[:, :, 7])
    every, to_west, to_east = lax.optimization_barrier((every, to_west, to_east))
    rows = lax.all_to_all(every, ("gx", "yz"), 0, 0)
    west = shifted(to_east, "gx", 1)
    east = shifted(to_west, "gx", -1)
    wide_vectors = jnp.concatenate(
        [west[:384].reshape(8, 3, 2, 8, 128), vectors, east[:384].reshape(8, 3, 2, 8, 128)], axis=2
    )
    wide_modulus = jnp.concatenate(
        [west[384:400].reshape(2, 8, 128), modulus, east[384:400].reshape(2, 8, 128)], axis=0
    )
    south = shifted(lines(wide_vectors[:, :, :, 6:8], wide_modulus[:, 6:8], residuals[:, :, :, 7]), "yz", 1)
    north = shifted(lines(wide_vectors[:, :, :, 0:2], wide_modulus[:, 0:2], residuals[:, :, :, 0]), "yz", -1)
    coeffs, near = solve_rows(spot, rows, count_x, count_y * width)
    result = local_parts(near, residuals, vectors, modulus, west, east, south, north)
    return (coeffs, result)


def solution(mesh):
    return jax.shard_map(
        on_device,
        mesh=mesh,
        in_specs=(
            P(None, None, "gx", "yz", None),
            P(None, None, "gx", "yz", None),
            P("gx", "yz", None),
            P(),
        ),
        out_specs=(P(("gx", "yz"), None), P(None, None, "gx", "yz", None)),
        check_vma=False,
    )
```

```python
import functools
import jax
import jax.numpy as jnp
from jax import lax
from jax.experimental import pallas as pl
from jax.experimental.pallas import tpu as pltpu
from jax.sharding import PartitionSpec as P

HIGH = lax.Precision.HIGHEST
GROUP = 5


def spread(values, column):
    return jnp.broadcast_to(values[:, column : column + 1], values.shape)


def fill(values, row):
    return jnp.broadcast_to(values[row : row + 1, :], values.shape)


def eliminate(work, picks, groups):
    row_index = lax.broadcasted_iota(jnp.int32, (8, 128), 0)

    def turn(step, carry):
        mats = [[work[pick, 8 * i : 8 * i + 8, :] for i in range(groups)] for pick in picks]
        for j in (0, 4):
            for mat in mats:
                cols = [[spread(mat[i], j + q) for q in range(4)] for i in range(groups)]
                r0, r1, r2, r3 = [fill(mat[0], j + q) for q in range(4)]
                p = [[fill(cols[0][q], j + i) for q in range(i + 1)] for i in range(4)]
                inverse = 1.0 / (p[0][0] * p[1][1] - p[1][0] * p[1][0])
                a0, a1, a2 = p[1][1] * inverse, -p[1][0] * inverse, p[0][0] * inverse
                y00 = p[2][0] * a0 + p[2][1] * a1
                y01 = p[2][0] * a1 + p[2][1] * a2
                y10 = p[3][0] * a0 + p[3][1] * a1
                y11 = p[3][0] * a1 + p[3][1] * a2
                s0 = p[2][2] - (y00 * p[2][0] + y01 * p[2][1])
                s1 = p[3][2] - (y10 * p[2][0] + y11 * p[2][1])
                s2 = p[3][3] - (y10 * p[3][0] + y11 * p[3][1])
                inverse = 1.0 / (s0 * s2 - s1 * s1)
                t2 = r2 - (y00 * r0 + y01 * r1)
                t3 = r3 - (y10 * r0 + y11 * r1)
                n2 = (s2 * t2 - s1 * t3) * inverse
                n3 = (s0 * t3 - s1 * t2) * inverse
                u0 = r0 - (p[2][0] * n2 + p[3][0] * n3)
                u1 = r1 - (p[2][1] * n2 + p[3][1] * n3)
                n0 = a0 * u0 + a1 * u1
                n1 = a1 * u0 + a2 * u1
                for i in range(groups):
                    changed = mat[i] - ((cols[i][0] * n0 + cols[i][1] * n1) + (cols[i][2] * n2 + cols[i][3] * n3))
                    if i == 0:
                        for q, new in enumerate((n0, n1, n2, n3)):
                            changed = jnp.where(row_index == j + q, new, changed)
                    mat[i] = changed
        for pick, mat in zip(picks, mats):
            for i in range(groups):
                to = (i + groups - 1) % groups
                work[pick, 8 * to : 8 * to + 8, :] = pltpu.roll(mat[i], 120, 1)
        return carry

    lax.fori_loop(0, groups, turn, 0)


def assemble(slabs, groups, rows_ref, work):
    lane = lax.broadcasted_iota(jnp.int32, (8, 128), 1)

    def within(start, width):
        return (lane >= start) & (lane < start + width)

    def slab(g, first):
        for h in range(groups):
            block = rows_ref[g * groups + h]
            mine = within(8 * h, min(16, 32 - 8 * h)) | within(64 + 8 * h, 8) | (lane >= 96)
            total = jnp.where(mine, block, 0.0)
            if h > 0:
                below = rows_ref[g * groups + h - 1]
                moved = pltpu.roll(below, 56, 1)
                extra = moved if h < 3 else pltpu.roll(below, 88, 1)
                total = total + jnp.where(within(8 * h - 8, 8), moved, jnp.where(within(8 * h, 8), extra, 0.0))
            if not first:
                before = rows_ref[(g - 1) * groups + h]
                moved = pltpu.roll(before, 88 if h < 3 else 120, 1)
                total = total + jnp.where(
                    within(8 * h, 8), moved, jnp.where(within(32 + 8 * h, 8), before, 0.0)
                )
            work[g, 8 * h : 8 * h + 8, :] = total

    slab(0, True)

    def later(g, carry):
        slab(g, False)
        return carry

    lax.fori_loop(1, slabs, later, 0)


def coarse_solve(slabs, size, chunk, spot, rows_ref, own_ref, near_ref, work, found):
    assemble(slabs, size // 8, rows_ref, work)
    lane = lax.broadcasted_iota(jnp.int32, (size, 128), 1)
    zeros = jnp.zeros((size, 128), jnp.float32)
    level = 1
    steps = []
    while level < slabs:
        picks = list(range(level, slabs, 2 * level))
        steps.append((level, picks))
        for at in range(0, len(picks), chunk):
            eliminate(work, picks[at : at + chunk], size // 8)
        for keep in range(0, slabs, 2 * level):
            own = work[keep]
            left, right = keep - level, keep + level
            before, after = zeros, zeros
            if left >= 0:
                block = work[left]
                before = jnp.where(
                    lane < size,
                    pltpu.roll(block, 128 - size, 1),
                    jnp.where((lane >= 2 * size) & (lane < 3 * size), 0.0, pltpu.roll(block, size, 1)),
                )
            if right < slabs:
                block = work[right]
                after = jnp.where(
                    lane < size, block, jnp.where(lane < 2 * size, 0.0, pltpu.roll(block, size, 1))
                )
            stack = jnp.concatenate([zeros, before, after, zeros], axis=0)
            change = jnp.dot(own, stack, precision=HIGH, preferred_element_type=jnp.float32)
            kept = jnp.where((lane >= size) & (lane < 3 * size), 0.0, own)
            work[keep] = kept - change
        level *= 2
    eliminate(work, [0], size // 8)
    found[...] = jnp.zeros(found.shape, jnp.float32)
    found[0] = jnp.where(lane < size, pltpu.roll(work[0], 128 - 2 * size, 1), 0.0)
    unit = jnp.where(lane == lax.broadcasted_iota(jnp.int32, (size, 128), 0), 1.0, 0.0)
    lowest = jnp.maximum(spot[0] - 1, 0)
    for level, picks in reversed(steps):
        first = lowest // level
        first = first + 1 - first % 2
        for wanted in (first, first + 2)[: len(picks)]:
            pick = jnp.minimum(wanted, slabs // level - 1) * level
            left, right = -found[pick - level], -found[pick + level]
            stack = jnp.concatenate([left, right, unit, zeros], axis=0)
            found[pick] = jnp.dot(work[pick], stack, precision=HIGH, preferred_element_type=jnp.float32)
    width = 128 - 3 * size

    def taken(slab, row):
        return found[slab, pl.ds(pl.multiple_of(row * 8, 8), 8), :][:, :width]

    own_ref[...] = taken(spot[0], spot[1])
    for step_x in range(3):
        for step_y in range(3):
            slab = jnp.clip(spot[0] + step_x - 1, 0, slabs - 1)
            row = jnp.clip(spot[1] + step_y - 1, 0, size // 8 - 1)
            at = (step_x * 3 + step_y) * 8
            near_ref[at : at + 8, :] = taken(slab, row)


def solve_rows(spot, rows, slabs, size, chunk=16):
    width = 128 - 3 * size
    whole = pl.BlockSpec(memory_space=pltpu.VMEM)
    return pl.pallas_call(
        functools.partial(coarse_solve, slabs, size, chunk),
        out_shape=(
            jax.ShapeDtypeStruct((8, width), jnp.float32),
            jax.ShapeDtypeStruct((72, width), jnp.float32),
        ),
        in_specs=[pl.BlockSpec(memory_space=pltpu.SMEM), whole],
        out_specs=(whole, whole),
        scratch_shapes=[
            pltpu.VMEM((slabs, size, 128), jnp.float32),
            pltpu.VMEM((slabs + 1, size, 128), jnp.float32),
        ],
        compiler_params=pltpu.CompilerParams(vmem_limit_bytes=16 * 1024 * 1024),
        cost_estimate=pl.CostEstimate(flops=20_000_000_000, bytes_accessed=90_000_000, transcendentals=0),
    )(spot, rows)


def panel_of(slots):
    lane = lax.broadcasted_iota(jnp.int32, (8, 128), 1)
    stack = jnp.concatenate([part for parts in slots for part in parts], axis=0)
    ones = jnp.ones((128, 128), jnp.float32)
    sums = jnp.dot(stack, ones, precision=HIGH, preferred_element_type=jnp.float32)
    columns = []
    at = 0
    for parts in slots:
        column = jnp.zeros((8, 128), jnp.float32)
        for k in range(len(parts)):
            column = jnp.where(lane == k, sums[at : at + 8], column)
            at += 8
        columns.append(column)
    return jnp.concatenate(columns, axis=0).T[:8]


def project(vec, res, out):
    def cell(index, totals):
        block = res[pl.ds(index, 32, stride=192), :]
        return tuple(totals[k] + block * vec[pl.ds(k * 192 + index, 1), :] for k in range(8))

    totals = lax.fori_loop(0, 192, cell, tuple(jnp.zeros((32, 128), jnp.float32) for _ in range(8)), unroll=4)
    slots = [[totals[k][8 * i : 8 * i + 8] for k in range(8)] for i in range(4)]
    out[...] = panel_of([[]] * 12 + slots)


def coarse_panel(spot, vec, modulus, east, north, known, out, rows, turned):
    lane = lax.broadcasted_iota(jnp.int32, (8, 128), 1)
    place = lax.broadcasted_iota(jnp.int32, (8, 128), 0)
    for x in range(8):
        centre = modulus[x]
        half = 0.5 * centre
        west = 0.5 * (centre + modulus[x - 1]) if x > 0 else half
        east_row = modulus[x + 1] if x < 7 else east[192:200, :]
        east_side = 0.5 * (centre + east_row)
        south = 0.5 * (centre + jnp.where(place == 0, 0.0, pltpu.roll(centre, 1, 0)))
        beyond = jnp.broadcast_to(north[192 + x : 193 + x, :], (8, 128))
        north_side = 0.5 * (centre + jnp.where(place == 7, beyond, pltpu.roll(centre, 7, 0)))
        lower = 0.5 * (centre + jnp.where(lane == 0, 0.0, pltpu.roll(centre, 1, 1)))
        upper = 0.5 * (centre + jnp.where(lane == 127, 0.0, pltpu.roll(centre, 127, 1)))
        span = slice(8 * x, 8 * x + 8)
        rows[0, span, :] = west if x > 0 else jnp.zeros((8, 128), jnp.float32)
        rows[1, span, :] = east_side if x < 7 else jnp.zeros((8, 128), jnp.float32)
        rows[2, span, :] = jnp.where(place == 0, 0.0, south)
        rows[3, span, :] = jnp.where(place == 7, 0.0, north_side)
        rows[4, span, :] = jnp.where(lane == 0, 0.0, lower)
        rows[5, span, :] = jnp.where(lane == 127, 0.0, upper)
        rows[6, span, :] = 0.002 + west + east_side + south + north_side + lower + upper
        rows[7, span, :] = east_side
        rows[8, span, :] = north_side

    def gather(index, carry):
        turned[index] = vec[pl.ds(index, 8, stride=192), :]
        return carry

    lax.fori_loop(0, 192, gather, 0, unroll=4)

    def own(index):
        return turned[index]

    zero = jnp.zeros((8, 128), jnp.float32)

    def cell(index, totals):
        at = index % 64
        weight = [rows[i, pl.ds(at, 1), :] for i in range(7)]
        here = own(index)
        applied = weight[6] * here - weight[4] * pltpu.roll(here, 1, 1) - weight[5] * pltpu.roll(here, 127, 1)
        applied = applied - weight[0] * own(jnp.maximum(index - 8, 0))
        applied = applied - weight[1] * own(jnp.minimum(index + 8, 191))
        applied = applied - weight[2] * own(jnp.maximum(index - 1, 0))
        applied = applied - weight[3] * own(jnp.minimum(index + 1, 191))
        return tuple(totals[k] + applied * vec[pl.ds(k * 192 + index, 1), :] for k in range(8))

    inside = lax.fori_loop(0, 192, cell, (zero,) * 8, unroll=8)

    def face(source, first, step, side):
        def spot_of(index, totals):
            comp, at = index // 8, index % 8
            cell_row = first + at * step
            mine = comp * 64 + cell_row
            weight = rows[side, pl.ds(cell_row, 1), :]
            half = 0.5 * modulus[cell_row // 8, pl.ds(cell_row % 8, 1), :]
            here = own(mine)
            there = source[pl.ds(index, 8, stride=24), :]
            toward, back, extra = -weight * there, -weight * here, half * there
            new = []
            for k in range(8):
                here_k = vec[pl.ds(k * 192 + mine, 1), :]
                there_k = source[pl.ds(k * 24 + index, 1), :]
                new += [
                    totals[3 * k] + toward * here_k,
                    totals[3 * k + 1] + back * there_k,
                    totals[3 * k + 2] + extra * there_k,
                ]
            return tuple(new)

        return lax.fori_loop(0, 24, spot_of, (zero,) * 24)

    easts = face(east, 56, 1, 7)
    norths = face(north, 7, 8, 8)

    panel = panel_of(
        [
            inside, norths[0::3], [], [],
            easts[1::3], easts[2::3], [], [],
            easts[0::3], norths[1::3], norths[2::3], [],
            [], [], [], [],
        ]
    )
    placed = panel
    for h in range(1, 4):
        ahead = pltpu.roll(panel, 8 * h, 1)
        behind = pltpu.roll(panel, 128 + 8 * h - 32, 1)
        moved = jnp.where(lane % 32 >= 8 * h, ahead, behind)
        placed = jnp.where(spot[1] == h, moved, placed)
    out[...] = jnp.broadcast_to((placed + known[...])[None], out.shape)


def coarse_rows(spot, residuals, vectors, modulus, east, north, count):
    whole = pl.BlockSpec(memory_space=pltpu.VMEM)
    vec = vectors.reshape(1536, 128)
    known = pl.pallas_call(
        project,
        out_shape=jax.ShapeDtypeStruct((8, 128), jnp.float32),
        in_specs=[whole, whole],
        out_specs=whole,
        compiler_params=pltpu.CompilerParams(vmem_limit_bytes=16 * 1024 * 1024),
        cost_estimate=pl.CostEstimate(flops=12_600_000, bytes_accessed=4_000_000, transcendentals=0),
    )(vec, residuals.reshape(6144, 128))
    return pl.pallas_call(
        coarse_panel,
        out_shape=jax.ShapeDtypeStruct((count, 8, 128), jnp.float32),
        in_specs=[pl.BlockSpec(memory_space=pltpu.SMEM)] + [whole] * 5,
        out_specs=whole,
        scratch_shapes=[pltpu.VMEM((9, 64, 128), jnp.float32), pltpu.VMEM((192, 8, 128), jnp.float32)],
        compiler_params=pltpu.CompilerParams(vmem_limit_bytes=16 * 1024 * 1024),
        cost_estimate=pl.CostEstimate(flops=6_000_000, bytes_accessed=2_000_000, transcendentals=0),
    )(spot, vec, modulus, east, north, known)


def sweep_rows(modulus, rows):
    lane = lax.broadcasted_iota(jnp.int32, (10, 128), 1)
    spot = lax.broadcasted_iota(jnp.int32, (10, 128), 0)
    for x in range(10):
        centre = modulus[x + 1, 1:11, :]
        west = 0.5 * (centre + modulus[x, 1:11, :])
        east = 0.5 * (centre + modulus[x + 2, 1:11, :])
        south = 0.5 * (centre + modulus[x + 1, 0:10, :])
        north = 0.5 * (centre + modulus[x + 1, 2:12, :])
        lower = 0.5 * (centre + jnp.where(lane == 0, 0.0, pltpu.roll(centre, 1, 1)))
        upper = 0.5 * (centre + jnp.where(lane == 127, 0.0, pltpu.roll(centre, 127, 1)))
        diagonal = 0.002 + west + east + south + north + lower + upper
        active = centre > 0
        if x in (0, 9):
            active = active & (spot > 0) & (spot < 9)
        scale = jnp.where(active, 0.8 / diagonal, 0.0)
        rows[0, x, 0:10, :] = west * scale
        rows[1, x, 0:10, :] = east * scale
        rows[2, x, 0:10, :] = south * scale
        rows[3, x, 0:10, :] = north * scale
        rows[4, x, 0:10, :] = jnp.where(lane == 0, 0.0, lower * scale)
        rows[5, x, 0:10, :] = jnp.where(lane == 127, 0.0, upper * scale)
        rows[6, x, 0:10, :] = scale


def local_stage(
    near_ref, res_far, vec, own_mod, west_far, east_far, south_far, north_far, out_far,
    modulus, rows, coeff, first, second, scaled, shift, res, west, east, south, north, out, arrived, left,
):
    pairs = ((west_far, west), (east_far, east), (south_far, south), (north_far, north), (res_far, res))
    loads = [pltpu.make_async_copy(far, here, arrived.at[n]) for n, (far, here) in enumerate(pairs)]
    for load in loads:
        load.start()

    near = near_ref[...]
    near = jnp.concatenate([near, jnp.zeros((72, 96), jnp.float32)], axis=1)
    near = jnp.concatenate([near, jnp.zeros((56, 128), jnp.float32)], axis=0)
    turned = near.T[:32]
    for index in range(72):
        coeff[index] = jnp.broadcast_to(turned[:, index : index + 1], (32, 128))

    def correct(near_index, cell, source, row_of, frozen):
        for comp in range(3):
            total = None
            for k in range(8):
                term = coeff[near_index * 8 + k] * source[pl.ds(row_of(k, comp), 1), :]
                total = term if total is None else total + term
            first[cell, comp * 32 : comp * 32 + 32, :] = total
            if frozen:
                second[cell, comp * 32 : comp * 32 + 32, :] = total

    def own_cell(index, carry):
        x, y = index // 8, index % 8
        correct(4, (x + 2) * 12 + y + 2, vec, lambda k, c: (k * 3 + c) * 64 + index, False)
        return carry

    lax.fori_loop(0, 64, own_cell, 0, unroll=2)

    for index in range(4):
        loads[index].wait()
    modulus[...] = jnp.zeros(modulus.shape, jnp.float32)
    modulus[2:10, 2:10, :] = own_mod[...]
    modulus[0:2, 2:10, :] = west[384:400, :].reshape(2, 8, 128)
    modulus[10:12, 2:10, :] = east[384:400, :].reshape(2, 8, 128)
    for x in range(8):
        modulus[x + 2, 0:2, :] = south[384 + 2 * x : 386 + 2 * x, :]
        modulus[x + 2, 10:12, :] = north[384 + 2 * x : 386 + 2 * x, :]
    for y, side in ((1, south), (10, north)):
        modulus[1, y : y + 1, :] = side[1192:1193, :]
        modulus[10, y : y + 1, :] = side[1217:1218, :]
    sweep_rows(modulus, rows)

    def edge_cells(y, carry):
        for layer in range(2):
            correct(1, layer * 12 + y + 2, west, lambda k, c: ((k * 3 + c) * 2 + layer) * 8 + y, layer == 0)
            correct(7, (10 + layer) * 12 + y + 2, east, lambda k, c: ((k * 3 + c) * 2 + layer) * 8 + y, layer == 1)
            correct(3, (y + 2) * 12 + layer, south, lambda k, c: ((k * 3 + c) * 8 + y) * 2 + layer, layer == 0)
            correct(5, (y + 2) * 12 + 10 + layer, north, lambda k, c: ((k * 3 + c) * 8 + y) * 2 + layer, layer == 1)
        return carry

    lax.fori_loop(0, 8, edge_cells, 0)
    for x, near_x, start in ((1, 0, 1168), (10, 6, 1193)):
        correct(near_x, x * 12 + 1, south, lambda k, c: start + k * 3 + c, True)
        correct(near_x + 2, x * 12 + 10, north, lambda k, c: start + k * 3 + c, True)
    loads[4].wait()

    def scale_cell(x, y, source, start, stride):
        weight = rows[6, x, pl.ds(y, 1), :]
        for comp in range(3):
            scaled[x * 10 + y, comp * 32 : comp * 32 + 32, :] = (
                source[pl.ds(start(comp), 32, stride=stride), :] * weight
            )

    def own_scaled(index, carry):
        x, y = index // 8, index % 8
        scale_cell(x + 1, y + 1, res, lambda c: c * 64 + index, 192)
        return carry

    lax.fori_loop(0, 64, own_scaled, 0, unroll=4)

    def edge_scaled(y, carry):
        scale_cell(0, y + 1, west, lambda c: 400 + c * 8 + y, 24)
        scale_cell(9, y + 1, east, lambda c: 400 + c * 8 + y, 24)
        scale_cell(y + 1, 0, south, lambda c: 400 + c * 8 + y, 24)
        scale_cell(y + 1, 9, north, lambda c: 400 + c * 8 + y, 24)
        return carry

    lax.fori_loop(0, 8, edge_scaled, 0, unroll=2)

    up = lax.broadcasted_iota(jnp.int32, (256, 256), 0) % 128
    to = lax.broadcasted_iota(jnp.int32, (256, 256), 1)
    moves = ((to < 128) & (to == up + 1)) | ((to >= 128) & (to - 128 == up - 1))
    shift[...] = jnp.where(moves, 1.0, 0.0).astype(jnp.bfloat16)

    def relax(x, y, cells, source, store):
        cell = (x + 1) * 12 + y + 1
        block = source[pl.ds(cell, cells)].reshape(cells * 96, 128)
        high = block.astype(jnp.bfloat16)
        rest = (block - high.astype(jnp.float32)).astype(jnp.bfloat16)
        moved = jnp.dot(
            jnp.concatenate([high, rest], axis=1), shift[...], preferred_element_type=jnp.float32
        )
        for n in range(cells):
            weight = [rows[i, x, pl.ds(y + n, 1), :] for i in range(6)]
            here = moved[n * 96 : n * 96 + 96]
            value = 0.2 * source[cell + n] + scaled[x * 10 + y + n]
            value = value + weight[0] * source[cell + n - 12] + weight[1] * source[cell + n + 12]
            value = value + weight[2] * source[cell + n - 1] + weight[3] * source[cell + n + 1]
            value = value + weight[4] * here[:, :128] + weight[5] * here[:, 128:]
            store(n, value)

    for source, target in ((first, second), (second, first), (first, second)):

        def sweep(x, y, cells, source=source, target=target):
            def keep(n, value):
                target[(x + 1) * 12 + y + n + 1] = value

            relax(x, y, cells, source, keep)

        def inner(index, carry, sweep=sweep):
            for y in range(0, 10, GROUP):
                sweep(index + 1, y, GROUP)
            return carry

        lax.fori_loop(0, 8, inner, 0)
        for x in (0, 9):
            for y in range(1, 9, 4):
                sweep(x, y, 4)

    def last(x, carry):
        for y in range(0, 8, 4):

            def keep(n, value, y=y):
                for comp in range(3):
                    out[pl.ds(comp * 64 + x * 8 + y + n, 32, stride=192), :] = value[comp * 32 : comp * 32 + 32]

            relax(x + 1, y + 1, 4, second, keep)
        slab(x).start()
        return carry

    def slab(x):
        return pltpu.make_async_copy(out.reshape(96, 8, 8, 128).at[:, x], out_far.at[:, x], left.at[x])

    lax.fori_loop(0, 8, last, 0)
    for x in range(8):
        slab(x).wait()


def local_parts(near, residuals, vectors, modulus, west, east, south, north):
    whole, far = pl.BlockSpec(memory_space=pltpu.VMEM), pl.BlockSpec(memory_space=pl.ANY)
    result = pl.pallas_call(
        local_stage,
        out_shape=jax.ShapeDtypeStruct((96, 8, 8, 128), jnp.float32),
        in_specs=[whole, far, whole, whole, far, far, far, far],
        out_specs=far,
        scratch_shapes=[
            pltpu.VMEM((12, 16, 128), jnp.float32),
            pltpu.VMEM((7, 10, 16, 128), jnp.float32),
            pltpu.VMEM((72, 32, 128), jnp.float32),
            pltpu.VMEM((144, 96, 128), jnp.float32),
            pltpu.VMEM((144, 96, 128), jnp.float32),
            pltpu.VMEM((100, 96, 128), jnp.float32),
            pltpu.VMEM((256, 256), jnp.bfloat16),
            pltpu.VMEM((6144, 128), jnp.float32),
            pltpu.VMEM((1168, 128), jnp.float32),
            pltpu.VMEM((1168, 128), jnp.float32),
            pltpu.VMEM((1218, 128), jnp.float32),
            pltpu.VMEM((1218, 128), jnp.float32),
            pltpu.VMEM((6144, 128), jnp.float32),
            pltpu.SemaphoreType.DMA((5,)),
            pltpu.SemaphoreType.DMA((8,)),
        ],
        compiler_params=pltpu.CompilerParams(vmem_limit_bytes=58 * 1024 * 1024),
    )(
        near,
        residuals.reshape(6144, 128),
        vectors.reshape(1536, 128),
        modulus,
        west,
        east,
        south,
        north,
    )
    return result.reshape(residuals.shape)

def shifted(values, axis, step):
    count = lax.axis_size(axis)
    return lax.ppermute(values, axis, [(i, i + step) for i in range(count) if 0 <= i + step < count])


def lines(*arrays):
    return jnp.concatenate([array.reshape(-1, 128) for array in arrays], axis=0)


def on_device(residuals, vectors, phases, stiffness):
    count_x = lax.axis_size("gx")
    count_y = lax.axis_size("yz")
    count = count_x * count_y
    index_x = lax.axis_index("gx")
    index_y = lax.axis_index("yz")
    width = vectors.shape[0]
    levels = stiffness.shape[0]
    choose = (phases[None] == jnp.arange(levels, dtype=jnp.int32)[:, None, None, None]).astype(
        jnp.float32
    )
    modulus = jnp.sum(stiffness[:, None, None, None] * choose, axis=0)
    east_face = shifted(lines(vectors[:, :, 0], modulus[0]), "gx", -1)
    north_face = shifted(lines(vectors[:, :, :, 0], modulus[:, 0]), "yz", -1)
    spot = jnp.stack([index_x, index_y]).astype(jnp.int32)
    every = coarse_rows(spot, residuals, vectors, modulus, east_face, north_face, count)
    to_west = lines(vectors[:, :, 0:2], modulus[0:2], residuals[:, :, 0])
    to_east = lines(vectors[:, :, 6:8], modulus[6:8], residuals[:, :, 7])
    every, to_west, to_east = lax.optimization_barrier((every, to_west, to_east))
    rows = lax.all_to_all(every, ("gx", "yz"), 0, 0)
    west = shifted(to_east, "gx", 1)
    east = shifted(to_west, "gx", -1)
    south = shifted(
        lines(vectors[:, :, :, 6:8], modulus[:, 6:8], residuals[:, :, :, 7], west[15:400:16], east[7:400:16]),
        "yz",
        1,
    )
    north = shifted(
        lines(vectors[:, :, :, 0:2], modulus[:, 0:2], residuals[:, :, :, 0], west[8:400:16], east[0:400:16]),
        "yz",
        -1,
    )
    coeffs, near = solve_rows(spot, rows, count_x, count_y * width)
    result = local_parts(near, residuals, vectors, modulus, west, east, south, north)
    return (coeffs, result)


def solution(mesh):
    return jax.shard_map(
        on_device,
        mesh=mesh,
        in_specs=(
            P(None, None, "gx", "yz", None),
            P(None, None, "gx", "yz", None),
            P("gx", "yz", None),
            P(),
        ),
        out_specs=(P(("gx", "yz"), None), P(None, None, "gx", "yz", None)),
        check_vma=False,
    )
```

```python
import functools
import jax
import jax.numpy as jnp
from jax import lax
from jax.experimental import pallas as pl
from jax.experimental.pallas import tpu as pltpu
from jax.sharding import PartitionSpec as P

HIGH = lax.Precision.HIGHEST
GROUP = 5


def spread(values, column):
    return jnp.broadcast_to(values[:, column : column + 1], values.shape)


def fill(values, row):
    return jnp.broadcast_to(values[row : row + 1, :], values.shape)


def eliminate(work, picks, groups):
    row_index = lax.broadcasted_iota(jnp.int32, (8, 128), 0)

    def turn(step, carry):
        mats = [[work[pick, 8 * i : 8 * i + 8, :] for i in range(groups)] for pick in picks]
        for j in (0, 4):
            for mat in mats:
                cols = [[spread(mat[i], j + q) for q in range(4)] for i in range(groups)]
                r0, r1, r2, r3 = [fill(mat[0], j + q) for q in range(4)]
                p = [[fill(cols[0][q], j + i) for q in range(i + 1)] for i in range(4)]
                inverse = 1.0 / (p[0][0] * p[1][1] - p[1][0] * p[1][0])
                a0, a1, a2 = p[1][1] * inverse, -p[1][0] * inverse, p[0][0] * inverse
                y00 = p[2][0] * a0 + p[2][1] * a1
                y01 = p[2][0] * a1 + p[2][1] * a2
                y10 = p[3][0] * a0 + p[3][1] * a1
                y11 = p[3][0] * a1 + p[3][1] * a2
                s0 = p[2][2] - (y00 * p[2][0] + y01 * p[2][1])
                s1 = p[3][2] - (y10 * p[2][0] + y11 * p[2][1])
                s2 = p[3][3] - (y10 * p[3][0] + y11 * p[3][1])
                inverse = 1.0 / (s0 * s2 - s1 * s1)
                t2 = r2 - (y00 * r0 + y01 * r1)
                t3 = r3 - (y10 * r0 + y11 * r1)
                n2 = (s2 * t2 - s1 * t3) * inverse
                n3 = (s0 * t3 - s1 * t2) * inverse
                u0 = r0 - (p[2][0] * n2 + p[3][0] * n3)
                u1 = r1 - (p[2][1] * n2 + p[3][1] * n3)
                n0 = a0 * u0 + a1 * u1
                n1 = a1 * u0 + a2 * u1
                for i in range(groups):
                    changed = mat[i] - ((cols[i][0] * n0 + cols[i][1] * n1) + (cols[i][2] * n2 + cols[i][3] * n3))
                    if i == 0:
                        for q, new in enumerate((n0, n1, n2, n3)):
                            changed = jnp.where(row_index == j + q, new, changed)
                    mat[i] = changed
        for pick, mat in zip(picks, mats):
            for i in range(groups):
                to = (i + groups - 1) % groups
                work[pick, 8 * to : 8 * to + 8, :] = pltpu.roll(mat[i], 120, 1)
        return carry

    lax.fori_loop(0, groups, turn, 0)


def assemble(slabs, groups, rows_ref, work):
    lane = lax.broadcasted_iota(jnp.int32, (8, 128), 1)

    def within(start, width):
        return (lane >= start) & (lane < start + width)

    def slab(g, first):
        for h in range(groups):
            block = rows_ref[g * groups + h]
            mine = within(8 * h, min(16, 32 - 8 * h)) | within(64 + 8 * h, 8) | (lane >= 96)
            total = jnp.where(mine, block, 0.0)
            if h > 0:
                below = rows_ref[g * groups + h - 1]
                moved = pltpu.roll(below, 56, 1)
                extra = moved if h < 3 else pltpu.roll(below, 88, 1)
                total = total + jnp.where(within(8 * h - 8, 8), moved, jnp.where(within(8 * h, 8), extra, 0.0))
            if not first:
                before = rows_ref[(g - 1) * groups + h]
                moved = pltpu.roll(before, 88 if h < 3 else 120, 1)
                total = total + jnp.where(
                    within(8 * h, 8), moved, jnp.where(within(32 + 8 * h, 8), before, 0.0)
                )
            work[g, 8 * h : 8 * h + 8, :] = total

    slab(0, True)

    def later(g, carry):
        slab(g, False)
        return carry

    lax.fori_loop(1, slabs, later, 0)


def coarse_solve(slabs, size, chunk, spot, rows_ref, own_ref, near_ref, work, found):
    assemble(slabs, size // 8, rows_ref, work)
    lane = lax.broadcasted_iota(jnp.int32, (size, 128), 1)
    zeros = jnp.zeros((size, 128), jnp.float32)
    level = 1
    steps = []
    while level < slabs:
        picks = list(range(level, slabs, 2 * level))
        steps.append((level, picks))
        for at in range(0, len(picks), chunk):
            eliminate(work, picks[at : at + chunk], size // 8)
        for keep in range(0, slabs, 2 * level):
            own = work[keep]
            left, right = keep - level, keep + level
            before, after = zeros, zeros
            if left >= 0:
                block = work[left]
                before = jnp.where(
                    lane < size,
                    pltpu.roll(block, 128 - size, 1),
                    jnp.where((lane >= 2 * size) & (lane < 3 * size), 0.0, pltpu.roll(block, size, 1)),
                )
            if right < slabs:
                block = work[right]
                after = jnp.where(
                    lane < size, block, jnp.where(lane < 2 * size, 0.0, pltpu.roll(block, size, 1))
                )
            stack = jnp.concatenate([zeros, before, after, zeros], axis=0)
            change = jnp.dot(own, stack, precision=HIGH, preferred_element_type=jnp.float32)
            kept = jnp.where((lane >= size) & (lane < 3 * size), 0.0, own)
            work[keep] = kept - change
        level *= 2
    eliminate(work, [0], size // 8)
    found[...] = jnp.zeros(found.shape, jnp.float32)
    found[0] = jnp.where(lane < size, pltpu.roll(work[0], 128 - 2 * size, 1), 0.0)
    unit = jnp.where(lane == lax.broadcasted_iota(jnp.int32, (size, 128), 0), 1.0, 0.0)
    lowest = jnp.maximum(spot[0] - 1, 0)
    for level, picks in reversed(steps):
        first = lowest // level
        first = first + 1 - first % 2
        for wanted in (first, first + 2)[: len(picks)]:
            pick = jnp.minimum(wanted, slabs // level - 1) * level
            left, right = -found[pick - level], -found[pick + level]
            stack = jnp.concatenate([left, right, unit, zeros], axis=0)
            found[pick] = jnp.dot(work[pick], stack, precision=HIGH, preferred_element_type=jnp.float32)
    width = 128 - 3 * size

    def taken(slab, row):
        return found[slab, pl.ds(pl.multiple_of(row * 8, 8), 8), :][:, :width]

    own_ref[...] = taken(spot[0], spot[1])
    for step_x in range(3):
        for step_y in range(3):
            slab = jnp.clip(spot[0] + step_x - 1, 0, slabs - 1)
            row = jnp.clip(spot[1] + step_y - 1, 0, size // 8 - 1)
            at = (step_x * 3 + step_y) * 8
            near_ref[at : at + 8, :] = taken(slab, row)


def solve_rows(spot, rows, slabs, size, chunk=16):
    width = 128 - 3 * size
    whole = pl.BlockSpec(memory_space=pltpu.VMEM)
    return pl.pallas_call(
        functools.partial(coarse_solve, slabs, size, chunk),
        out_shape=(
            jax.ShapeDtypeStruct((8, width), jnp.float32),
            jax.ShapeDtypeStruct((72, width), jnp.float32),
        ),
        in_specs=[pl.BlockSpec(memory_space=pltpu.SMEM), whole],
        out_specs=(whole, whole),
        scratch_shapes=[
            pltpu.VMEM((slabs, size, 128), jnp.float32),
            pltpu.VMEM((slabs + 1, size, 128), jnp.float32),
        ],
        compiler_params=pltpu.CompilerParams(vmem_limit_bytes=16 * 1024 * 1024),
        cost_estimate=pl.CostEstimate(flops=20_000_000_000, bytes_accessed=90_000_000, transcendentals=0),
    )(spot, rows)


def panel_of(slots):
    lane = lax.broadcasted_iota(jnp.int32, (8, 128), 1)
    stack = jnp.concatenate([part for parts in slots for part in parts], axis=0)
    ones = jnp.ones((128, 128), jnp.float32)
    sums = jnp.dot(stack, ones, precision=HIGH, preferred_element_type=jnp.float32)
    columns = []
    at = 0
    for parts in slots:
        column = jnp.zeros((8, 128), jnp.float32)
        for k in range(len(parts)):
            column = jnp.where(lane == k, sums[at : at + 8], column)
            at += 8
        columns.append(column)
    return jnp.concatenate(columns, axis=0).T[:8]


def project(vec, res, modulus, out, to_west, to_east, to_south, to_north):
    def cell(index, totals):
        block = res[pl.ds(index, 32, stride=192), :]
        return tuple(totals[k] + block * vec[pl.ds(k * 192 + index, 1), :] for k in range(8))

    totals = lax.fori_loop(0, 192, cell, tuple(jnp.zeros((32, 128), jnp.float32) for _ in range(8)), unroll=4)
    slots = [[totals[k][8 * i : 8 * i + 8] for k in range(8)] for i in range(4)]
    out[...] = panel_of([[]] * 12 + slots)

    def lines_of(index, carry):
        for side, first in ((to_west, 0), (to_east, 48)):
            side[pl.ds(pl.multiple_of(index * 16, 16), 16), :] = vec[pl.ds(pl.multiple_of(index * 64 + first, 16), 16), :]
        for side, first in ((to_south, 0), (to_north, 6)):
            for layer in range(2):
                side[pl.ds(pl.multiple_of(index * 16 + layer * 8, 8), 8), :] = vec[
                    pl.ds(index * 64 + first + layer, 8, stride=8), :
                ]
        at = pl.multiple_of(400 + index * 32, 16)
        start = index // 8 * 64
        place = index % 8
        to_west[pl.ds(at, 32), :] = res[pl.ds(start + place, 32, stride=192), :]
        to_east[pl.ds(at, 32), :] = res[pl.ds(start + 56 + place, 32, stride=192), :]
        to_south[pl.ds(at, 32), :] = res[pl.ds(start + place * 8, 32, stride=192), :]
        to_north[pl.ds(at, 32), :] = res[pl.ds(start + place * 8 + 7, 32, stride=192), :]
        return carry

    lax.fori_loop(0, 24, lines_of, 0, unroll=2)
    for layer in range(2):
        span = slice(384 + 8 * layer, 392 + 8 * layer)
        to_west[span, :] = modulus[layer]
        to_east[span, :] = modulus[6 + layer]
        for side, y in ((to_south, layer), (to_north, 6 + layer)):
            side[span, :] = jnp.concatenate([modulus[x, y : y + 1, :] for x in range(8)], axis=0)
    for side, edge in ((to_west, 0), (to_east, 7)):
        for start, y in ((1168, 7), (1200, 0)):
            side[start : start + 24, :] = vec[pl.ds(edge * 8 + y, 24, stride=64), :]
            side[start + 24 : start + 32, :] = modulus[edge]
    blank = jnp.zeros((64, 128), jnp.float32)
    to_south[1168:1232, :] = blank
    to_north[1168:1232, :] = blank


def coarse_panel(spot, vec, modulus, east, north, known, out, rows, turned):
    lane = lax.broadcasted_iota(jnp.int32, (8, 128), 1)
    place = lax.broadcasted_iota(jnp.int32, (8, 128), 0)
    for x in range(8):
        centre = modulus[x]
        half = 0.5 * centre
        west = 0.5 * (centre + modulus[x - 1]) if x > 0 else half
        east_row = modulus[x + 1] if x < 7 else east[192:200, :]
        east_side = 0.5 * (centre + east_row)
        south = 0.5 * (centre + jnp.where(place == 0, 0.0, pltpu.roll(centre, 1, 0)))
        beyond = jnp.broadcast_to(north[192 + x : 193 + x, :], (8, 128))
        north_side = 0.5 * (centre + jnp.where(place == 7, beyond, pltpu.roll(centre, 7, 0)))
        lower = 0.5 * (centre + jnp.where(lane == 0, 0.0, pltpu.roll(centre, 1, 1)))
        upper = 0.5 * (centre + jnp.where(lane == 127, 0.0, pltpu.roll(centre, 127, 1)))
        span = slice(8 * x, 8 * x + 8)
        rows[0, span, :] = west if x > 0 else jnp.zeros((8, 128), jnp.float32)
        rows[1, span, :] = east_side if x < 7 else jnp.zeros((8, 128), jnp.float32)
        rows[2, span, :] = jnp.where(place == 0, 0.0, south)
        rows[3, span, :] = jnp.where(place == 7, 0.0, north_side)
        rows[4, span, :] = jnp.where(lane == 0, 0.0, lower)
        rows[5, span, :] = jnp.where(lane == 127, 0.0, upper)
        rows[6, span, :] = 0.002 + west + east_side + south + north_side + lower + upper
        rows[7, span, :] = east_side
        rows[8, span, :] = north_side

    def gather(index, carry):
        turned[index] = vec[pl.ds(index, 8, stride=192), :]
        return carry

    lax.fori_loop(0, 192, gather, 0, unroll=4)

    def own(index):
        return turned[index]

    zero = jnp.zeros((8, 128), jnp.float32)

    def cell(index, totals):
        at = index % 64
        weight = [rows[i, pl.ds(at, 1), :] for i in range(7)]
        here = own(index)
        applied = weight[6] * here - weight[4] * pltpu.roll(here, 1, 1) - weight[5] * pltpu.roll(here, 127, 1)
        applied = applied - weight[0] * own(jnp.maximum(index - 8, 0))
        applied = applied - weight[1] * own(jnp.minimum(index + 8, 191))
        applied = applied - weight[2] * own(jnp.maximum(index - 1, 0))
        applied = applied - weight[3] * own(jnp.minimum(index + 1, 191))
        return tuple(totals[k] + applied * vec[pl.ds(k * 192 + index, 1), :] for k in range(8))

    inside = lax.fori_loop(0, 192, cell, (zero,) * 8, unroll=8)

    def face(source, first, step, side):
        def spot_of(index, totals):
            comp, at = index // 8, index % 8
            cell_row = first + at * step
            mine = comp * 64 + cell_row
            weight = rows[side, pl.ds(cell_row, 1), :]
            half = 0.5 * modulus[cell_row // 8, pl.ds(cell_row % 8, 1), :]
            here = own(mine)
            there = source[pl.ds(index, 8, stride=24), :]
            toward, back, extra = -weight * there, -weight * here, half * there
            new = []
            for k in range(8):
                here_k = vec[pl.ds(k * 192 + mine, 1), :]
                there_k = source[pl.ds(k * 24 + index, 1), :]
                new += [
                    totals[3 * k] + toward * here_k,
                    totals[3 * k + 1] + back * there_k,
                    totals[3 * k + 2] + extra * there_k,
                ]
            return tuple(new)

        return lax.fori_loop(0, 24, spot_of, (zero,) * 24)

    easts = face(east, 56, 1, 7)
    norths = face(north, 7, 8, 8)

    panel = panel_of(
        [
            inside, norths[0::3], [], [],
            easts[1::3], easts[2::3], [], [],
            easts[0::3], norths[1::3], norths[2::3], [],
            [], [], [], [],
        ]
    )
    placed = panel
    for h in range(1, 4):
        ahead = pltpu.roll(panel, 8 * h, 1)
        behind = pltpu.roll(panel, 128 + 8 * h - 32, 1)
        moved = jnp.where(lane % 32 >= 8 * h, ahead, behind)
        placed = jnp.where(spot[1] == h, moved, placed)
    out[...] = jnp.broadcast_to((placed + known[...])[None], out.shape)


def coarse_rows(spot, residuals, vectors, modulus, east, north, count):
    whole = pl.BlockSpec(memory_space=pltpu.VMEM)
    vec = vectors.reshape(1536, 128)
    message = jax.ShapeDtypeStruct((1232, 128), jnp.float32)
    known, *messages = pl.pallas_call(
        project,
        out_shape=(jax.ShapeDtypeStruct((8, 128), jnp.float32),) + (message,) * 4,
        in_specs=[whole] * 3,
        out_specs=(whole,) * 5,
        compiler_params=pltpu.CompilerParams(vmem_limit_bytes=16 * 1024 * 1024),
        cost_estimate=pl.CostEstimate(flops=12_600_000, bytes_accessed=4_000_000, transcendentals=0),
    )(vec, residuals.reshape(6144, 128), modulus)
    every = pl.pallas_call(
        coarse_panel,
        out_shape=jax.ShapeDtypeStruct((count, 8, 128), jnp.float32),
        in_specs=[pl.BlockSpec(memory_space=pltpu.SMEM)] + [whole] * 5,
        out_specs=whole,
        scratch_shapes=[pltpu.VMEM((9, 64, 128), jnp.float32), pltpu.VMEM((192, 8, 128), jnp.float32)],
        compiler_params=pltpu.CompilerParams(vmem_limit_bytes=16 * 1024 * 1024),
        cost_estimate=pl.CostEstimate(flops=6_000_000, bytes_accessed=2_000_000, transcendentals=0),
    )(spot, vec, modulus, east, north, known)
    return every, messages


def sweep_rows(modulus, rows):
    lane = lax.broadcasted_iota(jnp.int32, (10, 128), 1)
    spot = lax.broadcasted_iota(jnp.int32, (10, 128), 0)
    for x in range(10):
        centre = modulus[x + 1, 1:11, :]
        west = 0.5 * (centre + modulus[x, 1:11, :])
        east = 0.5 * (centre + modulus[x + 2, 1:11, :])
        south = 0.5 * (centre + modulus[x + 1, 0:10, :])
        north = 0.5 * (centre + modulus[x + 1, 2:12, :])
        lower = 0.5 * (centre + jnp.where(lane == 0, 0.0, pltpu.roll(centre, 1, 1)))
        upper = 0.5 * (centre + jnp.where(lane == 127, 0.0, pltpu.roll(centre, 127, 1)))
        diagonal = 0.002 + west + east + south + north + lower + upper
        active = centre > 0
        if x in (0, 9):
            active = active & (spot > 0) & (spot < 9)
        scale = jnp.where(active, 0.8 / diagonal, 0.0)
        rows[0, x, 0:10, :] = west * scale
        rows[1, x, 0:10, :] = east * scale
        rows[2, x, 0:10, :] = south * scale
        rows[3, x, 0:10, :] = north * scale
        rows[4, x, 0:10, :] = jnp.where(lane == 0, 0.0, lower * scale)
        rows[5, x, 0:10, :] = jnp.where(lane == 127, 0.0, upper * scale)
        rows[6, x, 0:10, :] = scale


def local_stage(
    near_ref, res_far, vec, own_mod, west_far, east_far, south_far, north_far, out_far,
    modulus, rows, coeff, first, second, scaled, shift, res, west, east, south, north, out, arrived, left,
):
    pairs = ((west_far, west), (east_far, east), (south_far, south), (north_far, north), (res_far, res))
    loads = [pltpu.make_async_copy(far, here, arrived.at[n]) for n, (far, here) in enumerate(pairs)]
    for load in loads:
        load.start()

    near = near_ref[...]
    near = jnp.concatenate([near, jnp.zeros((72, 96), jnp.float32)], axis=1)
    near = jnp.concatenate([near, jnp.zeros((56, 128), jnp.float32)], axis=0)
    turned = near.T[:32]
    for index in range(72):
        coeff[index] = jnp.broadcast_to(turned[:, index : index + 1], (32, 128))

    def correct(near_index, cell, source, row_of, frozen):
        for comp in range(3):
            total = None
            for k in range(8):
                term = coeff[near_index * 8 + k] * source[pl.ds(row_of(k, comp), 1), :]
                total = term if total is None else total + term
            first[cell, comp * 32 : comp * 32 + 32, :] = total
            if frozen:
                second[cell, comp * 32 : comp * 32 + 32, :] = total

    def own_cell(index, carry):
        x, y = index // 8, index % 8
        correct(4, (x + 2) * 12 + y + 2, vec, lambda k, c: (k * 3 + c) * 64 + index, False)
        return carry

    lax.fori_loop(0, 64, own_cell, 0, unroll=2)

    for index in range(4):
        loads[index].wait()
    modulus[...] = jnp.zeros(modulus.shape, jnp.float32)
    modulus[2:10, 2:10, :] = own_mod[...]
    modulus[0:2, 2:10, :] = west[384:400, :].reshape(2, 8, 128)
    modulus[10:12, 2:10, :] = east[384:400, :].reshape(2, 8, 128)
    for x in range(8):
        for layer in range(2):
            row = 384 + 8 * layer + x
            modulus[x + 2, layer : layer + 1, :] = south[row : row + 1, :]
            modulus[x + 2, 10 + layer : 11 + layer, :] = north[row : row + 1, :]
    for y, side, row in ((1, south, 1199), (10, north, 1192)):
        modulus[1, y : y + 1, :] = side[row : row + 1, :]
        modulus[10, y : y + 1, :] = side[row + 32 : row + 33, :]
    sweep_rows(modulus, rows)

    def edge_cells(y, carry):
        for layer in range(2):
            correct(1, layer * 12 + y + 2, west, lambda k, c: ((k * 3 + c) * 2 + layer) * 8 + y, layer == 0)
            correct(7, (10 + layer) * 12 + y + 2, east, lambda k, c: ((k * 3 + c) * 2 + layer) * 8 + y, layer == 1)
            correct(3, (y + 2) * 12 + layer, south, lambda k, c: (k * 3 + c) * 16 + layer * 8 + y, layer == 0)
            correct(5, (y + 2) * 12 + 10 + layer, north, lambda k, c: (k * 3 + c) * 16 + layer * 8 + y, layer == 1)
        return carry

    lax.fori_loop(0, 8, edge_cells, 0)
    for x, near_x, start in ((1, 0, 1168), (10, 6, 1200)):
        correct(near_x, x * 12 + 1, south, lambda k, c: start + k * 3 + c, True)
        correct(near_x + 2, x * 12 + 10, north, lambda k, c: start + k * 3 + c, True)
    loads[4].wait()

    def scale_cell(x, y, source, start, stride):
        weight = rows[6, x, pl.ds(y, 1), :]
        for comp in range(3):
            scaled[x * 10 + y, comp * 32 : comp * 32 + 32, :] = (
                (
                    source[pl.ds(start(comp), 32, stride=stride), :]
                    if stride > 1
                    else source[pl.ds(pl.multiple_of(start(comp), 16), 32), :]
                )
                * weight
            )

    def own_scaled(index, carry):
        x, y = index // 8, index % 8
        scale_cell(x + 1, y + 1, res, lambda c: c * 64 + index, 192)
        return carry

    lax.fori_loop(0, 64, own_scaled, 0, unroll=4)

    def edge_scaled(y, carry):
        scale_cell(0, y + 1, west, lambda c: 400 + (c * 8 + y) * 32, 1)
        scale_cell(9, y + 1, east, lambda c: 400 + (c * 8 + y) * 32, 1)
        scale_cell(y + 1, 0, south, lambda c: 400 + (c * 8 + y) * 32, 1)
        scale_cell(y + 1, 9, north, lambda c: 400 + (c * 8 + y) * 32, 1)
        return carry

    lax.fori_loop(0, 8, edge_scaled, 0, unroll=2)

    up = lax.broadcasted_iota(jnp.int32, (256, 256), 0) % 128
    to = lax.broadcasted_iota(jnp.int32, (256, 256), 1)
    moves = ((to < 128) & (to == up + 1)) | ((to >= 128) & (to - 128 == up - 1))
    shift[...] = jnp.where(moves, 1.0, 0.0).astype(jnp.bfloat16)

    def relax(x, y, cells, source, store):
        cell = (x + 1) * 12 + y + 1
        block = source[pl.ds(cell, cells)].reshape(cells * 96, 128)
        high = block.astype(jnp.bfloat16)
        rest = (block - high.astype(jnp.float32)).astype(jnp.bfloat16)
        moved = jnp.dot(
            jnp.concatenate([high, rest], axis=1), shift[...], preferred_element_type=jnp.float32
        )
        for n in range(cells):
            weight = [rows[i, x, pl.ds(y + n, 1), :] for i in range(6)]
            here = moved[n * 96 : n * 96 + 96]
            value = 0.2 * source[cell + n] + scaled[x * 10 + y + n]
            value = value + weight[0] * source[cell + n - 12] + weight[1] * source[cell + n + 12]
            value = value + weight[2] * source[cell + n - 1] + weight[3] * source[cell + n + 1]
            value = value + weight[4] * here[:, :128] + weight[5] * here[:, 128:]
            store(n, value)

    for source, target in ((first, second), (second, first), (first, second)):

        def sweep(x, y, cells, source=source, target=target):
            def keep(n, value):
                target[(x + 1) * 12 + y + n + 1] = value

            relax(x, y, cells, source, keep)

        def inner(index, carry, sweep=sweep):
            for y in range(0, 10, GROUP):
                sweep(index + 1, y, GROUP)
            return carry

        lax.fori_loop(0, 8, inner, 0)
        for x in (0, 9):
            for y in range(1, 9, 4):
                sweep(x, y, 4)

    def last(x, carry):
        for y in range(0, 8, 4):

            def keep(n, value, y=y):
                for comp in range(3):
                    out[pl.ds(comp * 64 + x * 8 + y + n, 32, stride=192), :] = value[comp * 32 : comp * 32 + 32]

            relax(x + 1, y + 1, 4, second, keep)
        slab(x).start()
        return carry

    def slab(x):
        return pltpu.make_async_copy(out.reshape(96, 8, 8, 128).at[:, x], out_far.at[:, x], left.at[x])

    lax.fori_loop(0, 8, last, 0)
    for x in range(8):
        slab(x).wait()


def local_parts(near, residuals, vectors, modulus, west, east, south, north):
    whole, far = pl.BlockSpec(memory_space=pltpu.VMEM), pl.BlockSpec(memory_space=pl.ANY)
    result = pl.pallas_call(
        local_stage,
        out_shape=jax.ShapeDtypeStruct((96, 8, 8, 128), jnp.float32),
        in_specs=[whole, far, whole, whole, far, far, far, far],
        out_specs=far,
        scratch_shapes=[
            pltpu.VMEM((12, 16, 128), jnp.float32),
            pltpu.VMEM((7, 10, 16, 128), jnp.float32),
            pltpu.VMEM((72, 32, 128), jnp.float32),
            pltpu.VMEM((144, 96, 128), jnp.float32),
            pltpu.VMEM((144, 96, 128), jnp.float32),
            pltpu.VMEM((100, 96, 128), jnp.float32),
            pltpu.VMEM((256, 256), jnp.bfloat16),
            pltpu.VMEM((6144, 128), jnp.float32),
            pltpu.VMEM((1232, 128), jnp.float32),
            pltpu.VMEM((1232, 128), jnp.float32),
            pltpu.VMEM((1232, 128), jnp.float32),
            pltpu.VMEM((1232, 128), jnp.float32),
            pltpu.VMEM((6144, 128), jnp.float32),
            pltpu.SemaphoreType.DMA((5,)),
            pltpu.SemaphoreType.DMA((8,)),
        ],
        compiler_params=pltpu.CompilerParams(vmem_limit_bytes=58 * 1024 * 1024),
    )(
        near,
        residuals.reshape(6144, 128),
        vectors.reshape(1536, 128),
        modulus,
        west,
        east,
        south,
        north,
    )
    return result.reshape(residuals.shape)

def shifted(values, axis, step):
    count = lax.axis_size(axis)
    return lax.ppermute(values, axis, [(i, i + step) for i in range(count) if 0 <= i + step < count])


def lines(*arrays):
    return jnp.concatenate([array.reshape(-1, 128) for array in arrays], axis=0)


def on_device(residuals, vectors, phases, stiffness):
    count_x = lax.axis_size("gx")
    count_y = lax.axis_size("yz")
    count = count_x * count_y
    index_x = lax.axis_index("gx")
    index_y = lax.axis_index("yz")
    width = vectors.shape[0]
    levels = stiffness.shape[0]
    choose = (phases[None] == jnp.arange(levels, dtype=jnp.int32)[:, None, None, None]).astype(
        jnp.float32
    )
    modulus = jnp.sum(stiffness[:, None, None, None] * choose, axis=0)
    east_face = shifted(lines(vectors[:, :, 0], modulus[0]), "gx", -1)
    north_face = shifted(lines(vectors[:, :, :, 0], modulus[:, 0]), "yz", -1)
    spot = jnp.stack([index_x, index_y]).astype(jnp.int32)
    every, messages = coarse_rows(spot, residuals, vectors, modulus, east_face, north_face, count)
    every, to_west, to_east, to_south, to_north = lax.optimization_barrier((every, *messages))
    rows = lax.all_to_all(every, ("gx", "yz"), 0, 0)
    west = shifted(to_east, "gx", 1)
    east = shifted(to_west, "gx", -1)
    to_north = to_north.at[1168:1200].set(west[1168:1200]).at[1200:1232].set(east[1168:1200])
    to_south = to_south.at[1168:1200].set(west[1200:1232]).at[1200:1232].set(east[1200:1232])
    south = shifted(to_north, "yz", 1)
    north = shifted(to_south, "yz", -1)
    coeffs, near = solve_rows(spot, rows, count_x, count_y * width)
    result = local_parts(near, residuals, vectors, modulus, west, east, south, north)
    return (coeffs, result)


def solution(mesh):
    return jax.shard_map(
        on_device,
        mesh=mesh,
        in_specs=(
            P(None, None, "gx", "yz", None),
            P(None, None, "gx", "yz", None),
            P("gx", "yz", None),
            P(),
        ),
        out_specs=(P(("gx", "yz"), None), P(None, None, "gx", "yz", None)),
        check_vma=False,
    )
```

```python
import functools
import jax
import jax.numpy as jnp
from jax import lax
from jax.experimental import pallas as pl
from jax.experimental.pallas import tpu as pltpu
from jax.sharding import PartitionSpec as P

HIGH = lax.Precision.HIGHEST
GROUP = 5


def spread(values, column):
    return jnp.broadcast_to(values[:, column : column + 1], values.shape)


def fill(values, row):
    return jnp.broadcast_to(values[row : row + 1, :], values.shape)


def eliminate(work, picks, groups):
    row_index = lax.broadcasted_iota(jnp.int32, (8, 128), 0)

    def turn(step, carry):
        mats = [[work[pick, 8 * i : 8 * i + 8, :] for i in range(groups)] for pick in picks]
        for j in (0, 4):
            for mat in mats:
                cols = [[spread(mat[i], j + q) for q in range(4)] for i in range(groups)]
                r0, r1, r2, r3 = [fill(mat[0], j + q) for q in range(4)]
                p = [[fill(cols[0][q], j + i) for q in range(i + 1)] for i in range(4)]
                inverse = 1.0 / (p[0][0] * p[1][1] - p[1][0] * p[1][0])
                a0, a1, a2 = p[1][1] * inverse, -p[1][0] * inverse, p[0][0] * inverse
                y00 = p[2][0] * a0 + p[2][1] * a1
                y01 = p[2][0] * a1 + p[2][1] * a2
                y10 = p[3][0] * a0 + p[3][1] * a1
                y11 = p[3][0] * a1 + p[3][1] * a2
                s0 = p[2][2] - (y00 * p[2][0] + y01 * p[2][1])
                s1 = p[3][2] - (y10 * p[2][0] + y11 * p[2][1])
                s2 = p[3][3] - (y10 * p[3][0] + y11 * p[3][1])
                inverse = 1.0 / (s0 * s2 - s1 * s1)
                t2 = r2 - (y00 * r0 + y01 * r1)
                t3 = r3 - (y10 * r0 + y11 * r1)
                n2 = (s2 * t2 - s1 * t3) * inverse
                n3 = (s0 * t3 - s1 * t2) * inverse
                u0 = r0 - (p[2][0] * n2 + p[3][0] * n3)
                u1 = r1 - (p[2][1] * n2 + p[3][1] * n3)
                n0 = a0 * u0 + a1 * u1
                n1 = a1 * u0 + a2 * u1
                for i in range(groups):
                    changed = mat[i] - ((cols[i][0] * n0 + cols[i][1] * n1) + (cols[i][2] * n2 + cols[i][3] * n3))
                    if i == 0:
                        for q, new in enumerate((n0, n1, n2, n3)):
                            changed = jnp.where(row_index == j + q, new, changed)
                    mat[i] = changed
        for pick, mat in zip(picks, mats):
            for i in range(groups):
                to = (i + groups - 1) % groups
                work[pick, 8 * to : 8 * to + 8, :] = pltpu.roll(mat[i], 120, 1)
        return carry

    lax.fori_loop(0, groups, turn, 0)


def assemble(slabs, groups, rows_ref, work):
    lane = lax.broadcasted_iota(jnp.int32, (8, 128), 1)

    def within(start, width):
        return (lane >= start) & (lane < start + width)

    def slab(g, first):
        for h in range(groups):
            block = rows_ref[g * groups + h]
            mine = within(8 * h, min(16, 32 - 8 * h)) | within(64 + 8 * h, 8) | (lane >= 96)
            total = jnp.where(mine, block, 0.0)
            if h > 0:
                below = rows_ref[g * groups + h - 1]
                moved = pltpu.roll(below, 56, 1)
                extra = moved if h < 3 else pltpu.roll(below, 88, 1)
                total = total + jnp.where(within(8 * h - 8, 8), moved, jnp.where(within(8 * h, 8), extra, 0.0))
            if not first:
                before = rows_ref[(g - 1) * groups + h]
                moved = pltpu.roll(before, 88 if h < 3 else 120, 1)
                total = total + jnp.where(
                    within(8 * h, 8), moved, jnp.where(within(32 + 8 * h, 8), before, 0.0)
                )
            work[g, 8 * h : 8 * h + 8, :] = total

    slab(0, True)

    def later(g, carry):
        slab(g, False)
        return carry

    lax.fori_loop(1, slabs, later, 0, unroll=4)


def coarse_solve(slabs, size, chunk, spot, rows_ref, own_ref, near_ref, work, found):
    assemble(slabs, size // 8, rows_ref, work)
    lane = lax.broadcasted_iota(jnp.int32, (size, 128), 1)
    zeros = jnp.zeros((size, 128), jnp.float32)
    level = 1
    steps = []
    while level < slabs:
        picks = list(range(level, slabs, 2 * level))
        steps.append((level, picks))
        for at in range(0, len(picks), chunk):
            eliminate(work, picks[at : at + chunk], size // 8)
        for keep in range(0, slabs, 2 * level):
            own = work[keep]
            left, right = keep - level, keep + level
            before, after = zeros, zeros
            if left >= 0:
                block = work[left]
                before = jnp.where(
                    lane < size,
                    pltpu.roll(block, 128 - size, 1),
                    jnp.where((lane >= 2 * size) & (lane < 3 * size), 0.0, pltpu.roll(block, size, 1)),
                )
            if right < slabs:
                block = work[right]
                after = jnp.where(
                    lane < size, block, jnp.where(lane < 2 * size, 0.0, pltpu.roll(block, size, 1))
                )
            stack = jnp.concatenate([zeros, before, after, zeros], axis=0)
            change = jnp.dot(own, stack, precision=HIGH, preferred_element_type=jnp.float32)
            kept = jnp.where((lane >= size) & (lane < 3 * size), 0.0, own)
            work[keep] = kept - change
        level *= 2
    eliminate(work, [0], size // 8)
    found[...] = jnp.zeros(found.shape, jnp.float32)
    found[0] = jnp.where(lane < size, pltpu.roll(work[0], 128 - 2 * size, 1), 0.0)
    unit = jnp.where(lane == lax.broadcasted_iota(jnp.int32, (size, 128), 0), 1.0, 0.0)
    lowest = jnp.maximum(spot[0] - 1, 0)
    for level, picks in reversed(steps):
        first = lowest // level
        first = first + 1 - first % 2
        for wanted in (first, first + 2)[: len(picks)]:
            pick = jnp.minimum(wanted, slabs // level - 1) * level
            left, right = -found[pick - level], -found[pick + level]
            stack = jnp.concatenate([left, right, unit, zeros], axis=0)
            found[pick] = jnp.dot(work[pick], stack, precision=HIGH, preferred_element_type=jnp.float32)
    width = 128 - 3 * size

    def taken(slab, row):
        return found[slab, pl.ds(pl.multiple_of(row * 8, 8), 8), :][:, :width]

    own_ref[...] = taken(spot[0], spot[1])
    for step_x in range(3):
        for step_y in range(3):
            slab = jnp.clip(spot[0] + step_x - 1, 0, slabs - 1)
            row = jnp.clip(spot[1] + step_y - 1, 0, size // 8 - 1)
            at = (step_x * 3 + step_y) * 8
            near_ref[at : at + 8, :] = taken(slab, row)


def solve_rows(spot, rows, slabs, size, chunk=16):
    width = 128 - 3 * size
    whole = pl.BlockSpec(memory_space=pltpu.VMEM)
    return pl.pallas_call(
        functools.partial(coarse_solve, slabs, size, chunk),
        out_shape=(
            jax.ShapeDtypeStruct((8, width), jnp.float32),
            jax.ShapeDtypeStruct((72, width), jnp.float32),
        ),
        in_specs=[pl.BlockSpec(memory_space=pltpu.SMEM), whole],
        out_specs=(whole, whole),
        scratch_shapes=[
            pltpu.VMEM((slabs, size, 128), jnp.float32),
            pltpu.VMEM((slabs + 1, size, 128), jnp.float32),
        ],
        compiler_params=pltpu.CompilerParams(vmem_limit_bytes=16 * 1024 * 1024),
        cost_estimate=pl.CostEstimate(flops=20_000_000_000, bytes_accessed=90_000_000, transcendentals=0),
    )(spot, rows)


def panel_of(slots):
    lane = lax.broadcasted_iota(jnp.int32, (8, 128), 1)
    stack = jnp.concatenate([part for parts in slots for part in parts], axis=0)
    ones = jnp.ones((128, 128), jnp.float32)
    sums = jnp.dot(stack, ones, precision=HIGH, preferred_element_type=jnp.float32)
    columns = []
    at = 0
    for parts in slots:
        column = jnp.zeros((8, 128), jnp.float32)
        for k in range(len(parts)):
            column = jnp.where(lane == k, sums[at : at + 8], column)
            at += 8
        columns.append(column)
    return jnp.concatenate(columns, axis=0).T[:8]


def project(vec, res, modulus, out, to_west, to_east, to_south, to_north):
    def cell(index, totals):
        block = res[pl.ds(index, 32, stride=192), :]
        return tuple(totals[k] + block * vec[pl.ds(k * 192 + index, 1), :] for k in range(8))

    totals = lax.fori_loop(0, 192, cell, tuple(jnp.zeros((32, 128), jnp.float32) for _ in range(8)), unroll=4)
    slots = [[totals[k][8 * i : 8 * i + 8] for k in range(8)] for i in range(4)]
    out[...] = panel_of([[]] * 12 + slots)

    def lines_of(index, carry):
        for side, first in ((to_west, 0), (to_east, 48)):
            side[pl.ds(pl.multiple_of(index * 16, 16), 16), :] = vec[pl.ds(pl.multiple_of(index * 64 + first, 16), 16), :]
        for side, first in ((to_south, 0), (to_north, 6)):
            for layer in range(2):
                side[pl.ds(pl.multiple_of(index * 16 + layer * 8, 8), 8), :] = vec[
                    pl.ds(index * 64 + first + layer, 8, stride=8), :
                ]
        at = pl.multiple_of(400 + index * 32, 16)
        start = index // 8 * 64
        place = index % 8
        to_west[pl.ds(at, 32), :] = res[pl.ds(start + place, 32, stride=192), :]
        to_east[pl.ds(at, 32), :] = res[pl.ds(start + 56 + place, 32, stride=192), :]
        to_south[pl.ds(at, 32), :] = res[pl.ds(start + place * 8, 32, stride=192), :]
        to_north[pl.ds(at, 32), :] = res[pl.ds(start + place * 8 + 7, 32, stride=192), :]
        return carry

    lax.fori_loop(0, 24, lines_of, 0, unroll=2)
    for layer in range(2):
        span = slice(384 + 8 * layer, 392 + 8 * layer)
        to_west[span, :] = modulus[layer]
        to_east[span, :] = modulus[6 + layer]
        for side, y in ((to_south, layer), (to_north, 6 + layer)):
            side[span, :] = jnp.concatenate([modulus[x, y : y + 1, :] for x in range(8)], axis=0)
    for side, edge in ((to_west, 0), (to_east, 7)):
        for start, y in ((1168, 7), (1200, 0)):
            side[start : start + 24, :] = vec[pl.ds(edge * 8 + y, 24, stride=64), :]
            side[start + 24 : start + 32, :] = modulus[edge]
    blank = jnp.zeros((64, 128), jnp.float32)
    to_south[1168:1232, :] = blank
    to_north[1168:1232, :] = blank


def coarse_panel(spot, vec, modulus, east, north, known, out, rows, turned):
    lane = lax.broadcasted_iota(jnp.int32, (8, 128), 1)
    place = lax.broadcasted_iota(jnp.int32, (8, 128), 0)
    for x in range(8):
        centre = modulus[x]
        half = 0.5 * centre
        west = 0.5 * (centre + modulus[x - 1]) if x > 0 else half
        east_row = modulus[x + 1] if x < 7 else east[192:200, :]
        east_side = 0.5 * (centre + east_row)
        south = 0.5 * (centre + jnp.where(place == 0, 0.0, pltpu.roll(centre, 1, 0)))
        beyond = jnp.broadcast_to(north[192 + x : 193 + x, :], (8, 128))
        north_side = 0.5 * (centre + jnp.where(place == 7, beyond, pltpu.roll(centre, 7, 0)))
        lower = 0.5 * (centre + jnp.where(lane == 0, 0.0, pltpu.roll(centre, 1, 1)))
        upper = 0.5 * (centre + jnp.where(lane == 127, 0.0, pltpu.roll(centre, 127, 1)))
        span = slice(8 * x, 8 * x + 8)
        rows[0, span, :] = west if x > 0 else jnp.zeros((8, 128), jnp.float32)
        rows[1, span, :] = east_side if x < 7 else jnp.zeros((8, 128), jnp.float32)
        rows[2, span, :] = jnp.where(place == 0, 0.0, south)
        rows[3, span, :] = jnp.where(place == 7, 0.0, north_side)
        rows[4, span, :] = jnp.where(lane == 0, 0.0, lower)
        rows[5, span, :] = jnp.where(lane == 127, 0.0, upper)
        rows[6, span, :] = 0.002 + west + east_side + south + north_side + lower + upper
        rows[7, span, :] = east_side
        rows[8, span, :] = north_side

    def gather(index, carry):
        turned[index] = vec[pl.ds(index, 8, stride=192), :]
        return carry

    lax.fori_loop(0, 192, gather, 0, unroll=4)

    def own(index):
        return turned[index]

    zero = jnp.zeros((8, 128), jnp.float32)

    def cell(index, totals):
        at = index % 64
        weight = [rows[i, pl.ds(at, 1), :] for i in range(7)]
        here = own(index)
        applied = weight[6] * here - weight[4] * pltpu.roll(here, 1, 1) - weight[5] * pltpu.roll(here, 127, 1)
        applied = applied - weight[0] * own(jnp.maximum(index - 8, 0))
        applied = applied - weight[1] * own(jnp.minimum(index + 8, 191))
        applied = applied - weight[2] * own(jnp.maximum(index - 1, 0))
        applied = applied - weight[3] * own(jnp.minimum(index + 1, 191))
        return tuple(totals[k] + applied * vec[pl.ds(k * 192 + index, 1), :] for k in range(8))

    inside = lax.fori_loop(0, 192, cell, (zero,) * 8, unroll=8)

    def face(source, first, step, side):
        def spot_of(index, totals):
            comp, at = index // 8, index % 8
            cell_row = first + at * step
            mine = comp * 64 + cell_row
            weight = rows[side, pl.ds(cell_row, 1), :]
            half = 0.5 * modulus[cell_row // 8, pl.ds(cell_row % 8, 1), :]
            here = own(mine)
            there = source[pl.ds(index, 8, stride=24), :]
            toward, back, extra = -weight * there, -weight * here, half * there
            new = []
            for k in range(8):
                here_k = vec[pl.ds(k * 192 + mine, 1), :]
                there_k = source[pl.ds(k * 24 + index, 1), :]
                new += [
                    totals[3 * k] + toward * here_k,
                    totals[3 * k + 1] + back * there_k,
                    totals[3 * k + 2] + extra * there_k,
                ]
            return tuple(new)

        return lax.fori_loop(0, 24, spot_of, (zero,) * 24, unroll=4)

    easts = face(east, 56, 1, 7)
    norths = face(north, 7, 8, 8)

    panel = panel_of(
        [
            inside, norths[0::3], [], [],
            easts[1::3], easts[2::3], [], [],
            easts[0::3], norths[1::3], norths[2::3], [],
            [], [], [], [],
        ]
    )
    placed = panel
    for h in range(1, 4):
        ahead = pltpu.roll(panel, 8 * h, 1)
        behind = pltpu.roll(panel, 128 + 8 * h - 32, 1)
        moved = jnp.where(lane % 32 >= 8 * h, ahead, behind)
        placed = jnp.where(spot[1] == h, moved, placed)
    out[...] = jnp.broadcast_to((placed + known[...])[None], out.shape)


def coarse_rows(spot, residuals, vectors, modulus, east, north, count):
    whole = pl.BlockSpec(memory_space=pltpu.VMEM)
    vec = vectors.reshape(1536, 128)
    message = jax.ShapeDtypeStruct((1232, 128), jnp.float32)
    known, *messages = pl.pallas_call(
        project,
        out_shape=(jax.ShapeDtypeStruct((8, 128), jnp.float32),) + (message,) * 4,
        in_specs=[whole] * 3,
        out_specs=(whole,) * 5,
        compiler_params=pltpu.CompilerParams(vmem_limit_bytes=16 * 1024 * 1024),
        cost_estimate=pl.CostEstimate(flops=12_600_000, bytes_accessed=4_000_000, transcendentals=0),
    )(vec, residuals.reshape(6144, 128), modulus)
    every = pl.pallas_call(
        coarse_panel,
        out_shape=jax.ShapeDtypeStruct((count, 8, 128), jnp.float32),
        in_specs=[pl.BlockSpec(memory_space=pltpu.SMEM)] + [whole] * 5,
        out_specs=whole,
        scratch_shapes=[pltpu.VMEM((9, 64, 128), jnp.float32), pltpu.VMEM((192, 8, 128), jnp.float32)],
        compiler_params=pltpu.CompilerParams(vmem_limit_bytes=16 * 1024 * 1024),
        cost_estimate=pl.CostEstimate(flops=6_000_000, bytes_accessed=2_000_000, transcendentals=0),
    )(spot, vec, modulus, east, north, known)
    return every, messages


def sweep_rows(modulus, rows):
    lane = lax.broadcasted_iota(jnp.int32, (10, 128), 1)
    spot = lax.broadcasted_iota(jnp.int32, (10, 128), 0)
    for x in range(10):
        centre = modulus[x + 1, 1:11, :]
        west = 0.5 * (centre + modulus[x, 1:11, :])
        east = 0.5 * (centre + modulus[x + 2, 1:11, :])
        south = 0.5 * (centre + modulus[x + 1, 0:10, :])
        north = 0.5 * (centre + modulus[x + 1, 2:12, :])
        lower = 0.5 * (centre + jnp.where(lane == 0, 0.0, pltpu.roll(centre, 1, 1)))
        upper = 0.5 * (centre + jnp.where(lane == 127, 0.0, pltpu.roll(centre, 127, 1)))
        diagonal = 0.002 + west + east + south + north + lower + upper
        active = centre > 0
        if x in (0, 9):
            active = active & (spot > 0) & (spot < 9)
        scale = jnp.where(active, 0.8 / diagonal, 0.0)
        rows[0, x, 0:10, :] = west * scale
        rows[1, x, 0:10, :] = east * scale
        rows[2, x, 0:10, :] = south * scale
        rows[3, x, 0:10, :] = north * scale
        rows[4, x, 0:10, :] = jnp.where(lane == 0, 0.0, lower * scale)
        rows[5, x, 0:10, :] = jnp.where(lane == 127, 0.0, upper * scale)
        rows[6, x, 0:10, :] = scale


def local_stage(
    near_ref, res_far, vec, own_mod, west_far, east_far, south_far, north_far, out_far,
    modulus, rows, coeff, first, second, scaled, shift, res, west, east, south, north, out, arrived, left,
):
    pairs = ((west_far, west), (east_far, east), (south_far, south), (north_far, north), (res_far, res))
    loads = [pltpu.make_async_copy(far, here, arrived.at[n]) for n, (far, here) in enumerate(pairs)]
    for load in loads:
        load.start()

    near = near_ref[...]
    near = jnp.concatenate([near, jnp.zeros((72, 96), jnp.float32)], axis=1)
    near = jnp.concatenate([near, jnp.zeros((56, 128), jnp.float32)], axis=0)
    turned = near.T[:32]
    for index in range(72):
        coeff[index] = jnp.broadcast_to(turned[:, index : index + 1], (32, 128))

    def correct(near_index, cell, source, row_of, frozen):
        for comp in range(3):
            total = None
            for k in range(8):
                term = coeff[near_index * 8 + k] * source[pl.ds(row_of(k, comp), 1), :]
                total = term if total is None else total + term
            first[cell, comp * 32 : comp * 32 + 32, :] = total
            if frozen:
                second[cell, comp * 32 : comp * 32 + 32, :] = total

    def own_cell(index, carry):
        x, y = index // 8, index % 8
        correct(4, (x + 2) * 12 + y + 2, vec, lambda k, c: (k * 3 + c) * 64 + index, False)
        return carry

    lax.fori_loop(0, 64, own_cell, 0, unroll=2)

    for index in range(4):
        loads[index].wait()
    modulus[...] = jnp.zeros(modulus.shape, jnp.float32)
    modulus[2:10, 2:10, :] = own_mod[...]
    modulus[0:2, 2:10, :] = west[384:400, :].reshape(2, 8, 128)
    modulus[10:12, 2:10, :] = east[384:400, :].reshape(2, 8, 128)
    for x in range(8):
        for layer in range(2):
            row = 384 + 8 * layer + x
            modulus[x + 2, layer : layer + 1, :] = south[row : row + 1, :]
            modulus[x + 2, 10 + layer : 11 + layer, :] = north[row : row + 1, :]
    for y, side, row in ((1, south, 1199), (10, north, 1192)):
        modulus[1, y : y + 1, :] = side[row : row + 1, :]
        modulus[10, y : y + 1, :] = side[row + 32 : row + 33, :]
    sweep_rows(modulus, rows)

    def edge_cells(y, carry):
        for layer in range(2):
            correct(1, layer * 12 + y + 2, west, lambda k, c: ((k * 3 + c) * 2 + layer) * 8 + y, layer == 0)
            correct(7, (10 + layer) * 12 + y + 2, east, lambda k, c: ((k * 3 + c) * 2 + layer) * 8 + y, layer == 1)
            correct(3, (y + 2) * 12 + layer, south, lambda k, c: (k * 3 + c) * 16 + layer * 8 + y, layer == 0)
            correct(5, (y + 2) * 12 + 10 + layer, north, lambda k, c: (k * 3 + c) * 16 + layer * 8 + y, layer == 1)
        return carry

    lax.fori_loop(0, 8, edge_cells, 0, unroll=2)
    for x, near_x, start in ((1, 0, 1168), (10, 6, 1200)):
        correct(near_x, x * 12 + 1, south, lambda k, c: start + k * 3 + c, True)
        correct(near_x + 2, x * 12 + 10, north, lambda k, c: start + k * 3 + c, True)
    loads[4].wait()

    def scale_cell(x, y, source, start, stride):
        weight = rows[6, x, pl.ds(y, 1), :]
        for comp in range(3):
            scaled[x * 10 + y, comp * 32 : comp * 32 + 32, :] = (
                (
                    source[pl.ds(start(comp), 32, stride=stride), :]
                    if stride > 1
                    else source[pl.ds(pl.multiple_of(start(comp), 16), 32), :]
                )
                * weight
            )

    def own_scaled(index, carry):
        x, y = index // 8, index % 8
        scale_cell(x + 1, y + 1, res, lambda c: c * 64 + index, 192)
        return carry

    lax.fori_loop(0, 64, own_scaled, 0, unroll=4)

    def edge_scaled(y, carry):
        scale_cell(0, y + 1, west, lambda c: 400 + (c * 8 + y) * 32, 1)
        scale_cell(9, y + 1, east, lambda c: 400 + (c * 8 + y) * 32, 1)
        scale_cell(y + 1, 0, south, lambda c: 400 + (c * 8 + y) * 32, 1)
        scale_cell(y + 1, 9, north, lambda c: 400 + (c * 8 + y) * 32, 1)
        return carry

    lax.fori_loop(0, 8, edge_scaled, 0, unroll=2)

    up = lax.broadcasted_iota(jnp.int32, (256, 256), 0) % 128
    to = lax.broadcasted_iota(jnp.int32, (256, 256), 1)
    moves = ((to < 128) & (to == up + 1)) | ((to >= 128) & (to - 128 == up - 1))
    shift[...] = jnp.where(moves, 1.0, 0.0).astype(jnp.bfloat16)

    def relax(x, y, cells, source, store):
        cell = (x + 1) * 12 + y + 1
        block = source[pl.ds(cell, cells)].reshape(cells * 96, 128)
        high = block.astype(jnp.bfloat16)
        rest = (block - high.astype(jnp.float32)).astype(jnp.bfloat16)
        moved = jnp.dot(
            jnp.concatenate([high, rest], axis=1), shift[...], preferred_element_type=jnp.float32
        )
        for n in range(cells):
            weight = [rows[i, x, pl.ds(y + n, 1), :] for i in range(6)]
            here = moved[n * 96 : n * 96 + 96]
            value = 0.2 * source[cell + n] + scaled[x * 10 + y + n]
            value = value + weight[0] * source[cell + n - 12] + weight[1] * source[cell + n + 12]
            value = value + weight[2] * source[cell + n - 1] + weight[3] * source[cell + n + 1]
            value = value + weight[4] * here[:, :128] + weight[5] * here[:, 128:]
            store(n, value)

    for source, target in ((first, second), (second, first), (first, second)):

        def sweep(x, y, cells, source=source, target=target):
            def keep(n, value):
                target[(x + 1) * 12 + y + n + 1] = value

            relax(x, y, cells, source, keep)

        def inner(index, carry, sweep=sweep):
            for y in range(0, 10, GROUP):
                sweep(index + 1, y, GROUP)
            return carry

        lax.fori_loop(0, 8, inner, 0)
        for x in (0, 9):
            for y in range(1, 9, 4):
                sweep(x, y, 4)

    def last(x, carry):
        for y in range(0, 8, 4):

            def keep(n, value, y=y):
                for comp in range(3):
                    out[pl.ds(comp * 64 + x * 8 + y + n, 32, stride=192), :] = value[comp * 32 : comp * 32 + 32]

            relax(x + 1, y + 1, 4, second, keep)
        slab(x).start()
        return carry

    def slab(x):
        return pltpu.make_async_copy(out.reshape(96, 8, 8, 128).at[:, x], out_far.at[:, x], left.at[x])

    lax.fori_loop(0, 8, last, 0)
    for x in range(8):
        slab(x).wait()


def local_parts(near, residuals, vectors, modulus, west, east, south, north):
    whole, far = pl.BlockSpec(memory_space=pltpu.VMEM), pl.BlockSpec(memory_space=pl.ANY)
    result = pl.pallas_call(
        local_stage,
        out_shape=jax.ShapeDtypeStruct((96, 8, 8, 128), jnp.float32),
        in_specs=[whole, far, whole, whole, far, far, far, far],
        out_specs=far,
        scratch_shapes=[
            pltpu.VMEM((12, 16, 128), jnp.float32),
            pltpu.VMEM((7, 10, 16, 128), jnp.float32),
            pltpu.VMEM((72, 32, 128), jnp.float32),
            pltpu.VMEM((144, 96, 128), jnp.float32),
            pltpu.VMEM((144, 96, 128), jnp.float32),
            pltpu.VMEM((100, 96, 128), jnp.float32),
            pltpu.VMEM((256, 256), jnp.bfloat16),
            pltpu.VMEM((6144, 128), jnp.float32),
            pltpu.VMEM((1232, 128), jnp.float32),
            pltpu.VMEM((1232, 128), jnp.float32),
            pltpu.VMEM((1232, 128), jnp.float32),
            pltpu.VMEM((1232, 128), jnp.float32),
            pltpu.VMEM((6144, 128), jnp.float32),
            pltpu.SemaphoreType.DMA((5,)),
            pltpu.SemaphoreType.DMA((8,)),
        ],
        compiler_params=pltpu.CompilerParams(vmem_limit_bytes=58 * 1024 * 1024),
    )(
        near,
        residuals.reshape(6144, 128),
        vectors.reshape(1536, 128),
        modulus,
        west,
        east,
        south,
        north,
    )
    return result.reshape(residuals.shape)

def shifted(values, axis, step):
    count = lax.axis_size(axis)
    return lax.ppermute(values, axis, [(i, i + step) for i in range(count) if 0 <= i + step < count])


def lines(*arrays):
    return jnp.concatenate([array.reshape(-1, 128) for array in arrays], axis=0)


def on_device(residuals, vectors, phases, stiffness):
    count_x = lax.axis_size("gx")
    count_y = lax.axis_size("yz")
    count = count_x * count_y
    index_x = lax.axis_index("gx")
    index_y = lax.axis_index("yz")
    width = vectors.shape[0]
    levels = stiffness.shape[0]
    choose = (phases[None] == jnp.arange(levels, dtype=jnp.int32)[:, None, None, None]).astype(
        jnp.float32
    )
    modulus = jnp.sum(stiffness[:, None, None, None] * choose, axis=0)
    east_face = shifted(lines(vectors[:, :, 0], modulus[0]), "gx", -1)
    north_face = shifted(lines(vectors[:, :, :, 0], modulus[:, 0]), "yz", -1)
    spot = jnp.stack([index_x, index_y]).astype(jnp.int32)
    every, messages = coarse_rows(spot, residuals, vectors, modulus, east_face, north_face, count)
    every, to_west, to_east, to_south, to_north = lax.optimization_barrier((every, *messages))
    rows = lax.all_to_all(every, ("gx", "yz"), 0, 0)
    west = shifted(to_east, "gx", 1)
    east = shifted(to_west, "gx", -1)
    to_north = to_north.at[1168:1200].set(west[1168:1200]).at[1200:1232].set(east[1168:1200])
    to_south = to_south.at[1168:1200].set(west[1200:1232]).at[1200:1232].set(east[1200:1232])
    south = shifted(to_north, "yz", 1)
    north = shifted(to_south, "yz", -1)
    coeffs, near = solve_rows(spot, rows, count_x, count_y * width)
    result = local_parts(near, residuals, vectors, modulus, west, east, south, north)
    return (coeffs, result)


def solution(mesh):
    return jax.shard_map(
        on_device,
        mesh=mesh,
        in_specs=(
            P(None, None, "gx", "yz", None),
            P(None, None, "gx", "yz", None),
            P("gx", "yz", None),
            P(),
        ),
        out_specs=(P(("gx", "yz"), None), P(None, None, "gx", "yz", None)),
        check_vma=False,
    )
```
